128 devices in a mesh: sub: 32 (over y, x, core), grp: 4 (over z).
Axes of the slice: x: 4, y: 4, z: 4, core: 2. Of those that a mesh axis runs over, the one named last changes fastest.
Arguments:
- jump_load: float32 [1024, 32, 128], P(('sub', 'grp'))
- local_inverse: bfloat16 [256, 1024, 1024], P(('sub', 'grp')), as said below
- dirichlet_schur: bfloat16 [256, 1024, 1024], P(('sub', 'grp')), as said below
- corner_coupling: bfloat16 [256, 192, 1024], P(('sub', 'grp')), may hold values from -0.25 to 0.25
- corner_map: int32 [256, 192], P(('sub', 'grp')), may hold values from 0 to 24575
- coarse_factor: bfloat16 [24576, 24576], P('grp', 'sub'), may hold values from -0.0390625 to 0.0390625
- block_links: int32 [128, 3, 8], P(('sub', 'grp')), may hold values from 0 to 15, as said below
- block_counts: int32 [128], P(('sub', 'grp')), may hold values from 6 to 8, as said below
Outputs:
- multipliers: float32 [1024, 32, 128], P(('sub', 'grp'))
- residual: float32 [1024, 32, 128], P(('sub', 'grp'))
- direction: float32 [1024, 32, 128], P(('sub', 'grp'))
The draws below stay inside these ranges and needn't reach their ends.
Inputs may be any that keep to these rules, and one draw needn't show every extreme that they name: block_counts[d] live slots on device d; at least one device has all 8 live. `block_links`: row 0: own block, row 1: side (1 to 4), row 2: block on that neighbour. Within a device the live own blocks are distinct, and no block is the own block or the far block of more than one live multiplier over all devices; no block is both. Each local_inverse[s] is symmetric positive definite. Each dirichlet_schur[s] is symmetric positive definite.
All inputs are finite; a program needn't handle non-finite values.
Results may differ from the reference program's by a relative error of at most 0.04.
Values may be sent and summed in bfloat16 or wider, within the bound.
No kernel may reach another device: no remote copies, remote signals or barrier semaphores. Data moves between devices by JAX's collectives and lax.ppermute only.
A program may use at most 128 MiB of HBM per device.

```python
import math
import jax
import jax.numpy as jnp
from jax import lax

I = 1024
BLK = 128
NB = 8
SUB_DEV = 2
NCS = 192
NC = 24576
K = 32
MCAP = 8
ITERS = 3
SUBS = 256
N_SUB = 32
N_GRP = 4


def definite(key, offset):
    noise_key, diagonal_key = jax.random.split(key)
    subdomains = SUB_DEV * N_SUB * N_GRP
    noise_field = jax.random.uniform(noise_key, (subdomains, I, I), jnp.float32, -0.02, 0.02)
    symmetric = 0.5 * (noise_field + jnp.swapaxes(noise_field, 1, 2))
    diagonal_mask = jnp.arange(I)[:, None] == jnp.arange(I)[None, :]
    diagonal = jax.random.uniform(diagonal_key, (subdomains, 1, I), jnp.float32, offset, offset + 1.0)
    return jnp.where(diagonal_mask[None], diagonal, symmetric).astype(jnp.bfloat16)


def draw_local_inverse(key, part):
    key = jax.random.fold_in(key, 31)
    return definite(key, 1.0)


def draw_dirichlet_schur(key, part):
    key = jax.random.fold_in(key, 37)
    return definite(key, 1.0)


def draw_jump_load(key, part):
    key = jax.random.fold_in(key, 7)
    value_key, row_key, column_key = jax.random.split(key, 3)
    rows_all = MCAP * N_SUB * N_GRP
    device_of = (jnp.arange(rows_all, dtype=jnp.int32) // MCAP).astype(jnp.float32)
    rising = 1.0 + 2.0 * device_of / max(N_SUB * N_GRP - 1, 1)
    row_scale = jnp.exp(jax.random.uniform(row_key, (rows_all,), jnp.float32, math.log(0.2), math.log(2.0)))
    column_scale = jnp.exp(jax.random.uniform(column_key, (K,), jnp.float32, math.log(0.4), math.log(1.2)))
    values = jax.random.normal(value_key, (rows_all, K, BLK), jnp.float32)
    return values * (rising * row_scale)[:, None, None] * column_scale[None, :, None]


def draw_block_links(key, part):
    key = jax.random.fold_in(key, 17)
    layout_key, own_key, slot_key = jax.random.split(key, 3)
    devices_all = N_SUB * N_GRP
    per_device = SUB_DEV * (I // BLK)
    halfway = per_device // 2
    layout = jax.vmap(lambda single: jax.random.permutation(single, per_device))(jax.random.split(layout_key, devices_all)).astype(jnp.int32)
    chosen = jax.vmap(lambda single: jax.random.permutation(single, halfway))(jax.random.split(own_key, devices_all))[:, :MCAP].astype(jnp.int32)
    slots = jax.vmap(lambda single: jax.random.permutation(single, 8))(jax.random.split(slot_key, devices_all))[:, :MCAP].astype(jnp.int32)
    own_blocks = jnp.take_along_axis(layout, chosen, axis=1)
    heading = 1 + slots // 2
    device_ids = jnp.arange(devices_all, dtype=jnp.int32)[:, None]
    step_sub = jnp.where(heading == 1, 1, 0) - jnp.where(heading == 2, 1, 0)
    step_grp = jnp.where(heading == 3, 1, 0) - jnp.where(heading == 4, 1, 0)
    sub_place = jnp.clip(device_ids // N_GRP + step_sub, 0, N_SUB - 1)
    grp_place = jnp.clip(device_ids % N_GRP + step_grp, 0, N_GRP - 1)
    target = sub_place * N_GRP + grp_place
    far_blocks = layout[target, halfway + slots]
    return jnp.stack([own_blocks, heading, far_blocks], axis=1).astype(jnp.int32)


def draw_block_counts(key, part):
    key = jax.random.fold_in(key, 23)
    count_key, heavy_key, full_key = jax.random.split(key, 3)
    devices_all = N_SUB * N_GRP
    drawn = jax.random.randint(count_key, (devices_all,), 6, 9, jnp.int32)
    heavy = jax.random.randint(heavy_key, (devices_all,), 0, 8, jnp.int32) == 0
    fullest = jax.random.randint(full_key, (), 0, devices_all, jnp.int32)
    filled = jnp.minimum(jnp.where(heavy, MCAP, drawn), MCAP)
    return jnp.where(jnp.arange(devices_all, dtype=jnp.int32) == fullest, MCAP, filled).astype(jnp.int32)


def place_ends(result, key, smallest, top_value):
    place = [jax.random.randint(jax.random.fold_in(key, axis), (), 0, length) for axis, length in enumerate(result.shape)]
    longest = result.shape.index(max(result.shape))
    next_to = place[:longest] + [(place[longest] + 1) % result.shape[longest]] + place[longest + 1:]
    return result.at[tuple(place)].set(smallest).at[tuple(next_to)].set(top_value)


def shard_levels(key, shape, cuts, low, high):
    factor_of, own = 1.0, jax.random.fold_in(key, 6)
    for dim, blocks in cuts:
        steps = jnp.exp(jax.random.uniform(jax.random.fold_in(own, dim), (blocks,), jnp.float32, low / len(cuts), high / len(cuts)))
        factor_of = factor_of * jnp.repeat(steps, shape[dim] // blocks).reshape([-1 if axis == dim else 1 for axis in range(len(shape))])
    return factor_of


def normal_values(rng, extent, scale, bound, shards=(), kind=jnp.bfloat16):
    values = scale * jax.random.normal(rng, extent, jnp.float32)
    if shards:
        values = values * shard_levels(rng, extent, shards, -0.22, 0.18)
    return jnp.clip(values, -bound, bound).astype(kind)


def setup_inputs(seed: int = 0) -> dict:
    keys = jax.random.split(jax.random.key(seed), 9)
    return {
        "jump_load": draw_jump_load(jax.random.fold_in(keys[8], 71), 0),
        "local_inverse": draw_local_inverse(jax.random.fold_in(keys[8], 71), 0),
        "dirichlet_schur": draw_dirichlet_schur(jax.random.fold_in(keys[8], 71), 0),
        "corner_coupling": normal_values(keys[3], (SUBS, NCS, I), (I // 2) ** -0.5, 0.25, ((0, 128),)),
        "corner_map": place_ends(jax.random.randint(keys[4], (SUBS, NCS), 0, NC), jax.random.fold_in(keys[4], 1), 0, NC - 1).astype(jnp.int32),
        "coarse_factor": normal_values(keys[5], (NC, NC), NC ** -0.5, 0.0390625, ((0, 4), (1, 32))),
        "block_links": draw_block_links(jax.random.fold_in(keys[8], 71), 0),
        "block_counts": draw_block_counts(jax.random.fold_in(keys[8], 71), 0),
    }


def link_data(block_links, block_counts):
    devices_all = block_links.shape[0]
    capacity = block_links.shape[2]
    device_ids = jnp.arange(devices_all, dtype=jnp.int32)[:, None]
    alive = jnp.arange(capacity, dtype=jnp.int32)[None, :] < block_counts[:, None]
    heading = block_links[:, 1, :]
    step_sub = jnp.where(heading == 1, 1, 0) - jnp.where(heading == 2, 1, 0)
    step_grp = jnp.where(heading == 3, 1, 0) - jnp.where(heading == 4, 1, 0)
    sub_place = device_ids // N_GRP + step_sub
    grp_place = device_ids % N_GRP + step_grp
    inside = (sub_place >= 0) & (sub_place < N_SUB) & (grp_place >= 0) & (grp_place < N_GRP)
    target = jnp.clip(sub_place, 0, N_SUB - 1) * N_GRP + jnp.clip(grp_place, 0, N_GRP - 1)
    per_device = SUB_DEV * NB
    own_rows = (device_ids * per_device + block_links[:, 0, :]).reshape(-1).astype(jnp.int32)
    far_rows = (target * per_device + block_links[:, 2, :]).reshape(-1).astype(jnp.int32)
    own_weight = alive.reshape(-1).astype(jnp.float32)[:, None, None]
    far_weight = (alive & inside).reshape(-1).astype(jnp.float32)[:, None, None]
    return own_rows, far_rows, own_weight, far_weight


def spread(values, links):
    own_rows, far_rows, own_weight, far_weight = links
    summed_up = jnp.zeros((SUBS * NB, K, BLK), jnp.float32)
    summed_up = summed_up.at[own_rows].add(values * own_weight).at[far_rows].add(-values * far_weight)
    return summed_up.reshape(SUBS, NB, K, BLK).transpose(0, 2, 1, 3).reshape(SUBS, K, I)


def jumps(surface, links):
    own_rows, far_rows, own_weight, far_weight = links
    pieces = surface.reshape(SUBS, K, NB, BLK).transpose(0, 2, 1, 3).reshape(SUBS * NB, K, BLK)
    return pieces[own_rows] * own_weight - pieces[far_rows] * far_weight


def right_product(operands):
    return jnp.dot(operands[0], operands[1], preferred_element_type=jnp.float32)


def transposed_product(operands):
    return lax.dot_general(operands[0], operands[1], (((1,), (1,)), ((), ())), preferred_element_type=jnp.float32)


def reference(jump_load, local_inverse, dirichlet_schur, corner_coupling, corner_map, coarse_factor, block_links, block_counts):
    links = link_data(block_links, block_counts)
    flat_map = corner_map.reshape(-1)

    def operator(direction):
        spread_in = spread(direction, links).astype(jnp.bfloat16)
        local_part = lax.map(right_product, (spread_in, local_inverse))
        corner_terms = lax.map(transposed_product, (spread_in, corner_coupling))
        assembled = jnp.zeros((K, NC), jnp.float32).at[:, flat_map].add(corner_terms.transpose(1, 0, 2).reshape(K, SUBS * NCS))
        forward = lax.dot_general(assembled.astype(jnp.bfloat16), coarse_factor, (((1,), (1,)), ((), ())), preferred_element_type=jnp.float32).astype(jnp.bfloat16)
        coarse = jnp.dot(forward, coarse_factor, preferred_element_type=jnp.float32).astype(jnp.bfloat16)
        picked = coarse[:, flat_map].reshape(K, SUBS, NCS).transpose(1, 0, 2)
        correction = lax.map(right_product, (picked, corner_coupling))
        return jumps(local_part + correction, links)

    def precondition(residual):
        spread_in = spread(residual, links).astype(jnp.bfloat16)
        return jumps(lax.map(right_product, (spread_in, dirichlet_schur)), links)

    residual = jump_load * links[2]
    multipliers = jnp.zeros_like(residual)
    precond = precondition(residual)
    direction = precond
    res_dot = jnp.sum(residual * precond, axis=(0, 2))
    for iteration in range(ITERS):
        applied = operator(direction)
        step_size = res_dot / jnp.sum(direction * applied, axis=(0, 2))
        multipliers = multipliers + step_size[None, :, None] * direction
        residual = residual - step_size[None, :, None] * applied
        precond = precondition(residual)
        new_dot = jnp.sum(residual * precond, axis=(0, 2))
        direction = precond + (new_dot / res_dot)[None, :, None] * direction
        res_dot = new_dot
    return multipliers, residual, direction
```

```python
import functools

import jax
import jax.numpy as jnp
from jax import lax
from jax.experimental import pallas as pl
from jax.experimental.pallas import tpu as pltpu
from jax.sharding import PartitionSpec as P

NC = 24576
ITERS = 3
CAP = 32
BOTH = ("sub", "grp")
BF16 = jnp.bfloat16
F32 = jnp.float32


NEIGHBOUR_SPOTS = ((2, 1), (0, 1), (1, 2), (1, 0))


def extended(array, sides, width):
    for axis, dim in sides:
        peers, length = (lax.axis_size(axis), array.shape[dim])
        up = [(i, (i + 1) % peers) for i in range(peers - 1)]
        down = [(j, i) for i, j in up]
        last = lax.slice_in_dim(array, length - width, length, axis=dim)
        first = lax.slice_in_dim(array, 0, width, axis=dim)
        before = lax.ppermute(last, axis, up)
        after = lax.ppermute(first, axis, down)
        array = jnp.concatenate([before, array, after], axis=dim)
    return array


def shortened(array):

    def short(part):
        return part.astype(jnp.bfloat16) if part.dtype == jnp.float32 else part

    return jax.tree.map(short, array)


def neighbours(padded):
    return [padded[position[0], position[1]] for position in NEIGHBOUR_SPOTS]


def general_path(
    jump_load,
    local_inverse,
    dirichlet_schur,
    corner_coupling,
    corner_map,
    coarse_factor,
    block_links,
    block_counts,
):
    capacity = jump_load.shape[0]
    loads = jump_load.shape[1]
    block_width = jump_load.shape[2]
    subdomains = local_inverse.shape[0]
    interface = local_inverse.shape[1]
    per_sub = interface // block_width
    primal = corner_coupling.shape[1]
    sub_cols = coarse_factor.shape[1]
    alive = jnp.arange(capacity, dtype=jnp.int32) < block_counts[0]
    own_blocks = block_links[0, 0]
    heading = jnp.where(alive, block_links[0, 1], 0)
    far_blocks = block_links[0, 2]
    own_weight = alive.astype(jnp.float32)[:, None, None]
    has_far = (heading > 0).astype(jnp.float32)[:, None, None]
    listing = jnp.stack([heading, far_blocks])
    listed = extended(listing[None, None], (("sub", 0), ("grp", 1)), 1)
    facing = jnp.array([2, 1, 4, 3], jnp.int32)
    near_lists = jnp.stack(neighbours(listed))
    in_rows = near_lists[:, 1, :].reshape(-1)
    in_weight = (
        (near_lists[:, 0, :] == facing[:, None]).astype(jnp.float32).reshape(-1)[:, None, None]
    )
    flat_map = corner_map.reshape(-1)

    def spread(values):
        padded = extended(shortened(values[None, None]), (("sub", 0), ("grp", 1)), 1)
        incoming = jnp.concatenate(neighbours(padded), axis=0)
        summed_up = jnp.zeros((subdomains, loads, per_sub, block_width), jnp.float32)
        summed_up = summed_up.at[own_blocks // per_sub, :, own_blocks % per_sub].add(
            values * own_weight
        )
        summed_up = summed_up.at[in_rows // per_sub, :, in_rows % per_sub].add(
            -incoming * in_weight
        )
        return summed_up.reshape(subdomains, loads, interface).astype(jnp.bfloat16)

    def jumps(surface):
        pieces = surface.reshape(subdomains, loads, per_sub, block_width)
        padded = extended(
            pieces[None, None].astype(jnp.bfloat16), (("sub", 0), ("grp", 1)), 1
        ).astype(jnp.float32)
        nearby = jnp.stack([pieces] + neighbours(padded))
        far_values = nearby[heading, far_blocks // per_sub, :, far_blocks % per_sub]
        own_values = pieces[own_blocks // per_sub, :, own_blocks % per_sub]
        return (own_values - far_values * has_far) * own_weight

    def precondition(residual):
        spread_in = spread(residual)
        return jumps(
            jnp.einsum(
                "ski,sij->skj", spread_in, dirichlet_schur, preferred_element_type=jnp.float32
            )
        )

    def column_sum(left, right):
        return jnp.sum(left * right, axis=(0, 2))

    def residual_products(residual, precond):
        return lax.psum(column_sum(residual, precond), ("sub", "grp"))

    residual = jump_load * own_weight
    multipliers = jnp.zeros_like(residual)
    precond = precondition(residual)
    direction = precond
    res_dot = residual_products(residual, precond)
    for iteration in range(ITERS):
        operator_spread_in = spread(direction)
        local_part = jnp.einsum(
            "ski,sij->skj", operator_spread_in, local_inverse, preferred_element_type=jnp.float32
        )
        corner_terms = jnp.einsum(
            "ski,sci->ksc", operator_spread_in, corner_coupling, preferred_element_type=jnp.float32
        )
        scattered = (
            jnp.zeros((loads, NC), jnp.float32)
            .at[:, flat_map]
            .add(corner_terms.reshape(loads, subdomains * primal))
        )
        summed = lax.psum(scattered, ("sub", "grp"))
        assembled = lax.dynamic_slice_in_dim(summed, lax.axis_index("sub") * sub_cols, sub_cols, 1)
        forward_part = lax.dot_general(
            assembled.astype(jnp.bfloat16),
            coarse_factor,
            (((1,), (1,)), ((), ())),
            preferred_element_type=jnp.float32,
        )
        forward = lax.psum(forward_part.astype(jnp.bfloat16), "sub")
        coarse_part = jnp.dot(forward, coarse_factor, preferred_element_type=jnp.float32)
        coarse = lax.psum(coarse_part.astype(jnp.bfloat16), "grp")
        coarse_all = lax.all_gather(coarse, "sub", axis=1, tiled=True)
        picked = coarse_all[:, flat_map].reshape(loads, subdomains, primal)
        correction = jnp.einsum(
            "ksc,sci->ski", picked, corner_coupling, preferred_element_type=jnp.float32
        )
        applied = jumps(local_part + correction)
        curvature = lax.psum(column_sum(direction, applied), ("sub", "grp"))
        step_size = res_dot / curvature
        multipliers = multipliers + step_size[None, :, None] * direction
        residual = residual - step_size[None, :, None] * applied
        precond = precondition(residual)
        new_dot = residual_products(residual, precond)
        direction = precond + (new_dot / res_dot)[None, :, None] * direction
        res_dot = new_dot
    return (multipliers, residual, direction)


def struct(shape, dtype):
    return jax.ShapeDtypeStruct(shape, dtype)


def params(**extra):
    return pltpu.CompilerParams(vmem_limit_bytes=48 * 1024 * 1024, **extra)


SMEM = pl.BlockSpec(memory_space=pltpu.SMEM)
VMEM = pl.BlockSpec(memory_space=pltpu.VMEM)


def matmul(left, right):
    return lax.dot_general(left, right, (((1,), (0,)), ((), ())), preferred_element_type=F32)


def matmul_t(left, right):
    return lax.dot_general(left, right, (((1,), (1,)), ((), ())), preferred_element_type=F32)


def from_neighbours(array):
    gathered = []
    for axis in BOTH:
        peers = lax.axis_size(axis)
        gathered.append(lax.ppermute(array, axis, [((i + 1) % peers, i) for i in range(peers)]))
        gathered.append(lax.ppermute(array, axis, [(i, (i + 1) % peers) for i in range(peers)]))
    return gathered


def exchange(array, axes):
    return lax.all_to_all(array, axes, 0, 0, tiled=True)


def tables_kernel(inside, own, near, jump, near1, near2, near3, near4, table, first):
    for block in range(16):
        for row in range(4):
            table[row, block] = 0
    first[...] = jnp.zeros_like(first)
    for m in range(8):
        block = own[m]

        @pl.when(own[8 + m] > 0)
        def _():
            side = own[8 + m]
            table[0, block] = jnp.where(inside[side - 1] > 0, side, 0)
            table[1, block] = own[16 + m]
            table[2, block] = 1
            table[3, block] = 1
            first[block] = jump[m]

    for side, facing, rows in ((1, 2, near1), (2, 1, near2), (3, 4, near3), (4, 3, near4)):
        for m in range(8):

            @pl.when((inside[side - 1] > 0) & (near[side - 1, 8 + m] == facing))
            def _():
                block = near[side - 1, 16 + m]
                table[0, block] = side
                table[1, block] = near[side - 1, m]
                table[2, block] = 1
                first[block] = -rows[pl.ds(m * 32, 32), :]


def set_up(jump, own, inside):
    rows = jnp.concatenate(
        [jump.reshape(256, 128), jnp.pad(own.astype(F32)[None, :], ((0, 7), (0, 104)))], axis=0
    )
    near = from_neighbours(rows)
    near_links = jnp.stack([n[256, :24] for n in near]).astype(jnp.int32)
    return pl.pallas_call(
        tables_kernel,
        out_shape=(struct((4, 16), jnp.int32), struct((16, 32, 128), F32)),
        in_specs=[SMEM, SMEM, SMEM] + [VMEM] * 5,
        out_specs=(SMEM, VMEM),
        compiler_params=params(),
    )(inside, own, near_links, jump, *near)


def halves(values):
    high = values.astype(BF16)
    return jnp.concatenate([high, (values - high.astype(F32)).astype(BF16)], axis=0)


def wide(ref, subdomain):
    return jnp.concatenate([ref[subdomain * 8 + j] for j in range(8)], axis=1)


def square_kernel(values, matrix, out):
    full = halves(jnp.concatenate([values[j] for j in range(8)], axis=1))
    got = matmul(full, matrix[0])
    got = got[:32] + got[32:]
    for j in range(out.shape[0]):
        out[j] = got[:, j * 128 : (j + 1) * 128]


def times_square(values, matrix):
    width = 512
    steps = 1024 // width
    return pl.pallas_call(
        square_kernel,
        grid=(2, steps),
        out_shape=struct((16, 32, 128), F32),
        in_specs=[
            pl.BlockSpec((8, 32, 128), lambda s, j: (s, 0, 0)),
            pl.BlockSpec((1, 1024, width), lambda s, j: (s, 0, j)),
        ],
        out_specs=pl.BlockSpec((width // 128, 32, 128), lambda s, j: (s * steps + j, 0, 0)),
        compiler_params=params(),
    )(values, matrix)


def jump_block(table, values, near, block):
    side, far = table[0, block], table[1, block]
    other = jnp.zeros((32, 128), F32)
    for k in range(4):
        other = jnp.where(side == k + 1, near[k][far].astype(F32), other)
    return jnp.where(table[2, block] > 0, values[block] - other, 0.0)


def jumps_kernel(table, values, near1, near2, near3, near4, out):
    for block in range(16):
        out[block] = jump_block(table, values, (near1, near2, near3, near4), block)


def jumps_of(table, values, near):
    return pl.pallas_call(
        jumps_kernel,
        out_shape=struct((16, 32, 128), F32),
        in_specs=[SMEM] + [VMEM] * 5,
        out_specs=VMEM,
        compiler_params=params(),
    )(table, values, *near)


def precondition(table, residual, schur):
    surface = times_square(residual, schur)
    return jumps_of(table, surface, from_neighbours(surface))


def lane_group():
    return lax.broadcasted_iota(jnp.int32, (8, 128), 1) // 32


def pick(lanes, parts, places):
    out = parts[0]
    for part, place in zip(parts[1:], places[1:]):
        out = jnp.where(lanes == place, part, out)
    return out


def turn(values, groups):
    groups = groups % 4
    return values if groups == 0 else pltpu.roll(values, groups * 32, 1)


def terms_kernel(grp, values, coupling, place, out):
    g = grp[0]
    lanes = lane_group()
    terms = []
    for s in range(2):
        got = matmul_t(halves(wide(values, s)), coupling[s])
        terms.append((got[:32] + got[32:]).astype(BF16))
    placed = matmul(terms[0], place[:192]) + matmul(terms[1], place[192:])
    at = [lax.rem(g + c, 4) for c in range(4)]
    for block in range(8):
        part = [placed[8 * i : 8 * i + 8, block * 128 : (block + 1) * 128] for i in range(4)]
        turned = [
            turn(pick(lanes, [part[(c + j) % 4] for c in range(4)], at), j) for j in range(4)
        ]
        for c in range(4):
            piece = pick(lanes, [turned[(i - c) % 4] for i in range(4)], at)
            row = (block * 4 + c) * 32
            out[pl.ds(row, 32), :] = jnp.concatenate([piece] * 4, axis=0).astype(BF16)


def forward_kernel(got, rows, factor, out, slots, assembled):
    step = pl.program_id(0)
    first = slots.shape[1] // rows.shape[0]

    @pl.when(step == 0)
    def _():
        lanes = lane_group()
        for s in range(32):
            part = got[pl.ds(s * 32, 32), :].astype(F32)
            part = [part[8 * c : 8 * c + 8] for c in range(4)]
            loads = [
                turn(pick(lanes, part, [(i + c) % 4 for c in range(4)]), -i) for i in range(4)
            ]
            slots[:, s * 128 : (s + 1) * 128] = jnp.concatenate(loads, axis=0).astype(BF16)
        assembled[...] = jnp.zeros_like(assembled)

    @pl.when(step < first)
    def _():
        size = rows.shape[0]
        at = pl.multiple_of(step * size, size)
        assembled[...] += matmul(slots[:, pl.ds(at, size)], rows[...])

    @pl.when(step >= first)
    def _():
        size = factor.shape[0]
        part = matmul_t(assembled[...].astype(BF16), factor[...]).astype(BF16)
        chunks = size // 128
        at = (step - first) * chunks
        for half in range(2):
            for j in range(chunks):
                row = pl.multiple_of((half * 48 + at + j) * 16, 16)
                out[pl.ds(row, 16), :] = part[16 * half : 16 * half + 16, j * 128 : j * 128 + 128]


def total_kernel(got, out):
    total = got[pl.ds(0, 48), :].astype(F32)
    for peer in range(1, 32):
        total += got[pl.ds(peer * 48, 48), :].astype(F32)
    total = total.astype(BF16)
    for peer in range(32):
        out[pl.ds(peer * 48, 48), :] = total


def coarse_kernel(got, factor, rows, out, solution):
    step = pl.program_id(0)
    size = factor.shape[0]
    chunks = size // 128
    first = 6144 // size

    @pl.when(step == 0)
    def _():
        solution[...] = jnp.zeros_like(solution)

    @pl.when(step < first)
    def _():
        halves_of = [
            [
                got[pl.ds(pl.multiple_of((half * 48 + step * chunks + j) * 16, 16), 16), :]
                for j in range(chunks)
            ]
            for half in range(2)
        ]
        forward = jnp.concatenate([jnp.concatenate(h, axis=1) for h in halves_of], axis=0)
        solution[...] += matmul(forward, factor[...])

    @pl.when(step >= first)
    def _():
        lanes = lane_group()
        picked = matmul_t(solution[...].astype(BF16), rows[...])
        groups = rows.shape[0] // 128
        for s in range(groups):
            part = [
                turn(picked[8 * i : 8 * i + 8, s * 128 : s * 128 + 128], i) for i in range(4)
            ]
            pieces = [pick(lanes, part, [(i + c) % 4 for i in range(4)]) for c in range(4)]
            row = pl.multiple_of(((step - first) * groups + s) * 32, 32)
            out[pl.ds(row, 32), :] = jnp.concatenate(pieces, axis=0).astype(BF16)


def correct_kernel(grp, got, place, coupling, local, out, picked):
    g = grp[0]
    lanes = lane_group()
    at = [lax.rem(g + c, 4) for c in range(4)]
    for block in range(8):
        sums = []
        for c in range(4):
            part = got[pl.ds((block * 4 + c) * 32, 32), :].astype(F32)
            sums.append(part[0:8] + part[8:16] + part[16:24] + part[24:32])
        turned = [
            turn(pick(lanes, [sums[(i - j) % 4] for i in range(4)], at), -j) for j in range(4)
        ]
        loads = [pick(lanes, [turned[(i - c) % 4] for c in range(4)], at) for i in range(4)]
        picked[:, block * 128 : (block + 1) * 128] = jnp.concatenate(loads, axis=0).astype(BF16)
    for s in range(2):
        values = matmul_t(picked[...], place[192 * s : 192 * s + 192]).astype(BF16)
        correction = matmul(values, coupling[s])
        for j in range(8):
            out[8 * s + j] = local[8 * s + j] + correction[:, 128 * j : 128 * j + 128]


def operate(table, direction, local_inverse, coupling, factor, place, rows, grp):
    sent = pl.pallas_call(
        terms_kernel,
        out_shape=struct((1024, 128), BF16),
        in_specs=[SMEM] + [VMEM] * 3,
        out_specs=VMEM,
        compiler_params=params(),
    )(grp, direction, coupling, place)
    got = exchange(sent, BOTH)
    local = times_square(direction, local_inverse)
    q_size, l_size = 1024, 512
    q_steps, l_steps = 4096 // q_size, 6144 // l_size
    partial = pl.pallas_call(
        forward_kernel,
        grid=(q_steps + l_steps,),
        out_shape=struct((1536, 128), BF16),
        in_specs=[
            pl.BlockSpec((1024, 128), lambda i: (0, 0)),
            pl.BlockSpec((q_size, 768), lambda i: (jnp.minimum(i, q_steps - 1), 0)),
            pl.BlockSpec((l_size, 768), lambda i: (jnp.maximum(i - q_steps, 0), 0)),
        ],
        out_specs=pl.BlockSpec((1536, 128), lambda i: (0, 0)),
        scratch_shapes=[pltpu.VMEM((32, 4096), BF16), pltpu.VMEM((32, 768), F32)],
        compiler_params=params(),
    )(got, rows, factor)
    got = exchange(partial, "sub")
    summed = pl.pallas_call(
        total_kernel,
        out_shape=struct((1536, 128), BF16),
        in_specs=[VMEM],
        out_specs=VMEM,
        compiler_params=params(),
    )(got)
    got = exchange(summed, "sub")
    coarse = pl.pallas_call(
        coarse_kernel,
        grid=(l_steps + q_steps,),
        out_shape=struct((1024, 128), BF16),
        in_specs=[
            pl.BlockSpec((1536, 128), lambda i: (0, 0)),
            pl.BlockSpec((l_size, 768), lambda i: (jnp.minimum(i, l_steps - 1), 0)),
            pl.BlockSpec((q_size, 768), lambda i: (jnp.maximum(i - l_steps, 0), 0)),
        ],
        out_specs=pl.BlockSpec((1024, 128), lambda i: (0, 0)),
        scratch_shapes=[pltpu.VMEM((32, 768), F32)],
        compiler_params=params(),
    )(got, factor, rows)
    got = exchange(coarse, BOTH)
    surface = pl.pallas_call(
        correct_kernel,
        out_shape=struct((16, 32, 128), F32),
        in_specs=[SMEM] + [VMEM] * 4,
        out_specs=VMEM,
        scratch_shapes=[pltpu.VMEM((32, 1024), BF16)],
        compiler_params=params(),
    )(grp, got, place, coupling, local)
    return jumps_of(table, surface, from_neighbours(surface))


def dots_kernel(table, *refs):
    out = refs[-1]
    pairs = [(refs[2 * i], refs[2 * i + 1]) for i in range((len(refs) - 1) // 2)]
    lanes = lax.broadcasted_iota(jnp.int32, (32, 128), 1)
    load = lax.broadcasted_iota(jnp.int32, (32, 128), 0)
    row = jnp.zeros((32, 128), F32)
    for i, (left, right) in enumerate(pairs):
        total = jnp.zeros((32, 128), F32)
        for block in range(16):
            total += jnp.where(table[3, block] > 0, left[block] * right[block], 0.0)
        row += jnp.where(lanes == load + 32 * i, jnp.sum(total, axis=1, keepdims=True), 0.0)
    out[...] = jnp.broadcast_to(jnp.sum(row, axis=0, keepdims=True), out.shape)


def products(table, pairs):
    flat = [array for pair in pairs for array in pair]
    sent = pl.pallas_call(
        dots_kernel,
        out_shape=struct((128, 128), F32),
        in_specs=[SMEM] + [VMEM] * len(flat),
        out_specs=VMEM,
        compiler_params=params(),
    )(table, *flat)
    return exchange(sent, BOTH)


def dots_of(got, count):
    total = jnp.sum(got[...], axis=0, keepdims=True)
    lanes = lax.broadcasted_iota(jnp.int32, (32, 128), 1)
    load = lax.broadcasted_iota(jnp.int32, (32, 128), 0)
    return [
        jnp.sum(jnp.where(lanes == load + 32 * i, total, 0.0), axis=1, keepdims=True)
        for i in range(count)
    ]


def first_update_kernel(got, r, u, w, m, x_out, r_out, u_out, kept):
    gamma, delta = dots_of(got, 2)
    alpha = gamma / delta
    kept[0] = jnp.broadcast_to(gamma, (32, 128))
    kept[1] = jnp.broadcast_to(delta, (32, 128))
    for b in range(16):
        x_out[b] = alpha * u[b]
        r_out[b] = r[b] - alpha * w[b]
        u_out[b] = u[b] - alpha * m[b]


def update_kernel(
    got, old, x, r, u, w, m, d, s, q, x_out, r_out, u_out, d_out, s_out, q_out, kept
):
    gamma, uw, us, dw = dots_of(got, 4)
    beta = gamma / old[0][:, 0:1]
    delta = uw + beta * (us + dw) + beta * beta * old[1][:, 0:1]
    alpha = gamma / delta
    kept[0] = jnp.broadcast_to(gamma, (32, 128))
    kept[1] = jnp.broadcast_to(delta, (32, 128))
    for b in range(16):
        dn = u[b] + beta * d[b]
        sn = w[b] + beta * s[b]
        qn = m[b] + beta * q[b]
        d_out[b] = dn
        s_out[b] = sn
        q_out[b] = qn
        x_out[b] = x[b] + alpha * dn
        r_out[b] = r[b] - alpha * sn
        u_out[b] = u[b] - alpha * qn


def finish_kernel(own, got, old, x, r, u, d, x_out, r_out, d_out):
    (gamma,) = dots_of(got, 1)
    beta = gamma / old[0][:, 0:1]
    for m in range(8):
        block = own[m]
        live = own[8 + m] > 0
        x_out[m] = jnp.where(live, x[block], 0.0)
        r_out[m] = jnp.where(live, r[block], 0.0)
        d_out[m] = jnp.where(live, u[block] + beta * d[block], 0.0)


FULL = struct((16, 32, 128), F32)
KEPT = struct((2, 32, 128), F32)


def fast_path(jump, local_inverse, schur, coupling, factor, own, inside, place, columns):
    grp = lax.axis_index("grp").astype(jnp.int32).reshape(1)
    rows = (columns.reshape(4096, 1) == jnp.arange(768, dtype=jnp.int32)[None, :]).astype(BF16)
    table, r = set_up(jump, own, inside)
    u = precondition(table, r, schur)
    for step in range(ITERS):
        w = operate(table, u, local_inverse, coupling, factor, place, rows, grp)
        if step == 0:
            got = products(table, [(r, u), (u, w)])
            m = precondition(table, w, schur)
            d, s, q = u, w, m
            x, r, u, kept = pl.pallas_call(
                first_update_kernel,
                out_shape=(FULL, FULL, FULL, KEPT),
                compiler_params=params(),
            )(got, r, u, w, m)
        else:
            got = products(table, [(r, u), (u, w), (u, s), (d, w)])
            m = precondition(table, w, schur)
            x, r, u, d, s, q, kept = pl.pallas_call(
                update_kernel,
                out_shape=(FULL,) * 6 + (KEPT,),
                compiler_params=params(),
            )(got, kept, x, r, u, w, m, d, s, q)
    got = products(table, [(r, u)])
    return pl.pallas_call(
        finish_kernel,
        out_shape=(struct((8, 32, 128), F32),) * 3,
        in_specs=[SMEM] + [VMEM] * 6,
        compiler_params=params(),
    )(own, got, kept, x, r, u, d)


def on_device(
    jump_load,
    local_inverse,
    dirichlet_schur,
    corner_coupling,
    corner_map,
    coarse_factor,
    block_links,
    block_counts,
):
    sub_cols = coarse_factor.shape[1]
    n_sub, n_grp = lax.axis_size("sub"), lax.axis_size("grp")
    sub, grp = lax.axis_index("sub"), lax.axis_index("grp")
    flat_map = corner_map.reshape(-1)
    block = flat_map // sub_cols
    column = flat_map - block * sub_cols
    order = jnp.arange(flat_map.shape[0], dtype=jnp.int32)
    before = (block[:, None] == block[None, :]) & (order[None, :] < order[:, None])
    rank = jnp.sum(before.astype(jnp.int32), axis=1)
    slot = block * CAP + rank
    fits = rank < CAP
    lane = (block // 4) * 128 + ((block + grp) % 4) * CAP + rank
    slots = jnp.arange(n_sub * CAP, dtype=jnp.int32)
    place = ((lane[:, None] == slots[None, :]) & fits[:, None]).astype(BF16)
    filled = jnp.where((slot[:, None] == slots[None, :]) & fits[:, None], column[:, None] + 1, 0)
    filled = jnp.sum(filled, axis=0).reshape(n_sub, CAP) - 1
    spilled = jnp.any(~fits).astype(jnp.int32)
    listing = jnp.concatenate([filled, jnp.full((n_sub, 128 - CAP), spilled, jnp.int32)], axis=1)
    listing = jnp.broadcast_to(listing[:, None, :], (n_sub, n_grp, 128)).reshape(-1, 128)
    listing = exchange(listing, BOTH)
    columns = listing[:, :CAP]
    spills = jnp.any(listing[:, CAP] > 0)
    alive = jnp.arange(8, dtype=jnp.int32) < block_counts[0]
    own = jnp.concatenate(
        [block_links[0, 0], jnp.where(alive, block_links[0, 1], 0), block_links[0, 2]]
    )
    inside = jnp.stack([sub < n_sub - 1, sub > 0, grp < n_grp - 1, grp > 0]).astype(jnp.int32)
    return lax.cond(
        spills,
        lambda: general_path(
            jump_load,
            local_inverse,
            dirichlet_schur,
            corner_coupling,
            corner_map,
            coarse_factor,
            block_links,
            block_counts,
        ),
        lambda: fast_path(
            jump_load,
            local_inverse,
            dirichlet_schur,
            corner_coupling,
            coarse_factor,
            own,
            inside,
            place,
            columns,
        ),
    )


def solution(mesh):
    in_specs = (
        P(("sub", "grp"), None, None),
        P(("sub", "grp"), None, None),
        P(("sub", "grp"), None, None),
        P(("sub", "grp"), None, None),
        P(("sub", "grp"), None),
        P("grp", "sub"),
        P(("sub", "grp"), None, None),
        P(("sub", "grp")),
    )
    out_specs = (
        P(("sub", "grp"), None, None),
        P(("sub", "grp"), None, None),
        P(("sub", "grp"), None, None),
    )
    return jax.shard_map(
        on_device, mesh=mesh, in_specs=in_specs, out_specs=out_specs, check_vma=False
    )
```

```python
import functools

import jax
import jax.numpy as jnp
from jax import lax
from jax.experimental import pallas as pl
from jax.experimental.pallas import tpu as pltpu
from jax.sharding import PartitionSpec as P

NC = 24576
ITERS = 3
CAP = 32
BOTH = ("sub", "grp")
BF16 = jnp.bfloat16
F32 = jnp.float32


NEIGHBOUR_SPOTS = ((2, 1), (0, 1), (1, 2), (1, 0))


def extended(array, sides, width):
    for axis, dim in sides:
        peers, length = (lax.axis_size(axis), array.shape[dim])
        up = [(i, (i + 1) % peers) for i in range(peers - 1)]
        down = [(j, i) for i, j in up]
        last = lax.slice_in_dim(array, length - width, length, axis=dim)
        first = lax.slice_in_dim(array, 0, width, axis=dim)
        before = lax.ppermute(last, axis, up)
        after = lax.ppermute(first, axis, down)
        array = jnp.concatenate([before, array, after], axis=dim)
    return array


def shortened(array):

    def short(part):
        return part.astype(jnp.bfloat16) if part.dtype == jnp.float32 else part

    return jax.tree.map(short, array)


def neighbours(padded):
    return [padded[position[0], position[1]] for position in NEIGHBOUR_SPOTS]


def general_path(
    jump_load,
    local_inverse,
    dirichlet_schur,
    corner_coupling,
    corner_map,
    coarse_factor,
    block_links,
    block_counts,
):
    capacity = jump_load.shape[0]
    loads = jump_load.shape[1]
    block_width = jump_load.shape[2]
    subdomains = local_inverse.shape[0]
    interface = local_inverse.shape[1]
    per_sub = interface // block_width
    primal = corner_coupling.shape[1]
    sub_cols = coarse_factor.shape[1]
    alive = jnp.arange(capacity, dtype=jnp.int32) < block_counts[0]
    own_blocks = block_links[0, 0]
    heading = jnp.where(alive, block_links[0, 1], 0)
    far_blocks = block_links[0, 2]
    own_weight = alive.astype(jnp.float32)[:, None, None]
    has_far = (heading > 0).astype(jnp.float32)[:, None, None]
    listing = jnp.stack([heading, far_blocks])
    listed = extended(listing[None, None], (("sub", 0), ("grp", 1)), 1)
    facing = jnp.array([2, 1, 4, 3], jnp.int32)
    near_lists = jnp.stack(neighbours(listed))
    in_rows = near_lists[:, 1, :].reshape(-1)
    in_weight = (
        (near_lists[:, 0, :] == facing[:, None]).astype(jnp.float32).reshape(-1)[:, None, None]
    )
    flat_map = corner_map.reshape(-1)

    def spread(values):
        padded = extended(shortened(values[None, None]), (("sub", 0), ("grp", 1)), 1)
        incoming = jnp.concatenate(neighbours(padded), axis=0)
        summed_up = jnp.zeros((subdomains, loads, per_sub, block_width), jnp.float32)
        summed_up = summed_up.at[own_blocks // per_sub, :, own_blocks % per_sub].add(
            values * own_weight
        )
        summed_up = summed_up.at[in_rows // per_sub, :, in_rows % per_sub].add(
            -incoming * in_weight
        )
        return summed_up.reshape(subdomains, loads, interface).astype(jnp.bfloat16)

    def jumps(surface):
        pieces = surface.reshape(subdomains, loads, per_sub, block_width)
        padded = extended(
            pieces[None, None].astype(jnp.bfloat16), (("sub", 0), ("grp", 1)), 1
        ).astype(jnp.float32)
        nearby = jnp.stack([pieces] + neighbours(padded))
        far_values = nearby[heading, far_blocks // per_sub, :, far_blocks % per_sub]
        own_values = pieces[own_blocks // per_sub, :, own_blocks % per_sub]
        return (own_values - far_values * has_far) * own_weight

    def precondition(residual):
        spread_in = spread(residual)
        return jumps(
            jnp.einsum(
                "ski,sij->skj", spread_in, dirichlet_schur, preferred_element_type=jnp.float32
            )
        )

    def column_sum(left, right):
        return jnp.sum(left * right, axis=(0, 2))

    def residual_products(residual, precond):
        return lax.psum(column_sum(residual, precond), ("sub", "grp"))

    residual = jump_load * own_weight
    multipliers = jnp.zeros_like(residual)
    precond = precondition(residual)
    direction = precond
    res_dot = residual_products(residual, precond)
    for iteration in range(ITERS):
        operator_spread_in = spread(direction)
        local_part = jnp.einsum(
            "ski,sij->skj", operator_spread_in, local_inverse, preferred_element_type=jnp.float32
        )
        corner_terms = jnp.einsum(
            "ski,sci->ksc", operator_spread_in, corner_coupling, preferred_element_type=jnp.float32
        )
        scattered = (
            jnp.zeros((loads, NC), jnp.float32)
            .at[:, flat_map]
            .add(corner_terms.reshape(loads, subdomains * primal))
        )
        summed = lax.psum(scattered, ("sub", "grp"))
        assembled = lax.dynamic_slice_in_dim(summed, lax.axis_index("sub") * sub_cols, sub_cols, 1)
        forward_part = lax.dot_general(
            assembled.astype(jnp.bfloat16),
            coarse_factor,
            (((1,), (1,)), ((), ())),
            preferred_element_type=jnp.float32,
        )
        forward = lax.psum(forward_part.astype(jnp.bfloat16), "sub")
        coarse_part = jnp.dot(forward, coarse_factor, preferred_element_type=jnp.float32)
        coarse = lax.psum(coarse_part.astype(jnp.bfloat16), "grp")
        coarse_all = lax.all_gather(coarse, "sub", axis=1, tiled=True)
        picked = coarse_all[:, flat_map].reshape(loads, subdomains, primal)
        correction = jnp.einsum(
            "ksc,sci->ski", picked, corner_coupling, preferred_element_type=jnp.float32
        )
        applied = jumps(local_part + correction)
        curvature = lax.psum(column_sum(direction, applied), ("sub", "grp"))
        step_size = res_dot / curvature
        multipliers = multipliers + step_size[None, :, None] * direction
        residual = residual - step_size[None, :, None] * applied
        precond = precondition(residual)
        new_dot = residual_products(residual, precond)
        direction = precond + (new_dot / res_dot)[None, :, None] * direction
        res_dot = new_dot
    return (multipliers, residual, direction)


def struct(shape, dtype):
    return jax.ShapeDtypeStruct(shape, dtype)


def cost(flops, size):
    return pl.CostEstimate(flops=flops, bytes_accessed=size, transcendentals=0)


def params(mib=16):
    return pltpu.CompilerParams(vmem_limit_bytes=mib * 1024 * 1024)


SMEM = pl.BlockSpec(memory_space=pltpu.SMEM)
VMEM = pl.BlockSpec(memory_space=pltpu.VMEM)
ANY = pl.BlockSpec(memory_space=pl.ANY)


def matmul(left, right):
    return lax.dot_general(left, right, (((1,), (0,)), ((), ())), preferred_element_type=F32)


def matmul_t(left, right):
    return lax.dot_general(left, right, (((1,), (1,)), ((), ())), preferred_element_type=F32)


def from_neighbours(array):
    gathered = []
    for axis in BOTH:
        peers = lax.axis_size(axis)
        gathered.append(lax.ppermute(array, axis, [((i + 1) % peers, i) for i in range(peers)]))
        gathered.append(lax.ppermute(array, axis, [(i, (i + 1) % peers) for i in range(peers)]))
    return gathered


def exchange(array, axes):
    return lax.all_to_all(array, axes, 0, 0, tiled=True)


def halves(values):
    high = values.astype(BF16)
    return jnp.concatenate([high, (values - high.astype(F32)).astype(BF16)], axis=0)


def wide(ref, subdomain):
    return jnp.concatenate([ref[subdomain * 8 + j] for j in range(8)], axis=1)


def square_copies(matrix, held, arrived):
    copies = [pltpu.make_async_copy(matrix.at[s], held.at[s], arrived.at[s]) for s in range(2)]
    for copy in copies:
        copy.start()
    return copies


def square(values, copies, held, out, sent=None):
    for s in range(2):
        full = halves(wide(values, s))
        copies[s].wait()
        got = matmul(full, held[s])
        got = got[:32] + got[32:]
        for j in range(8):
            block = got[:, j * 128 : j * 128 + 128]
            out[8 * s + j] = block
            if sent is not None:
                sent[8 * s + j] = block.astype(BF16)


SQUARE = [pltpu.VMEM((2, 1024, 1024), BF16), pltpu.SemaphoreType.DMA((2,))]
FULL = struct((16, 32, 128), F32)
OWN = struct((8, 32, 128), F32)
SENT = struct((16, 32, 128), BF16)


def first_kernel(
    inside, own, near, jump, near1, near2, near3, near4, matrix, table, r, out, sent, first, held, arrived
):
    copies = square_copies(matrix, held, arrived)
    for block in range(16):
        for row in range(4):
            table[row, block] = 0
        table[4, block] = inside[4]
        table[5, block] = own[block % 8]
        table[6, block] = (own[8 + block % 8] > 0).astype(jnp.int32)
    first[...] = jnp.zeros_like(first)
    r[...] = jnp.zeros_like(r)
    for m in range(8):
        block = own[m]

        @pl.when(own[8 + m] > 0)
        def _():
            side = own[8 + m]
            table[0, block] = jnp.where(inside[side - 1] > 0, side, 0)
            table[1, block] = own[16 + m]
            table[2, block] = 1
            table[3, block] = 1
            first[block] = jump[m]
            r[m] = jump[m]

    for side, facing, rows in ((1, 2, near1), (2, 1, near2), (3, 4, near3), (4, 3, near4)):
        for m in range(8):

            @pl.when((inside[side - 1] > 0) & (near[side - 1, 8 + m] == facing))
            def _():
                block = near[side - 1, 16 + m]
                table[0, block] = side
                table[1, block] = near[side - 1, m]
                table[2, block] = 1
                first[block] = -rows[pl.ds(m * 32, 32), :]

    square(first, copies, held, out, sent)


def set_up(jump, own, inside, matrix):
    rows = jnp.concatenate(
        [jump.reshape(256, 128), jnp.pad(own.astype(F32)[None, :], ((0, 7), (0, 104)))], axis=0
    )
    near = from_neighbours(rows)
    near_links = jnp.stack([n[256, :24] for n in near]).astype(jnp.int32)
    return pl.pallas_call(
        first_kernel,
        out_shape=(struct((7, 16), jnp.int32), OWN, FULL, SENT),
        in_specs=[SMEM, SMEM, SMEM] + [VMEM] * 5 + [ANY],
        out_specs=(SMEM, VMEM, VMEM, VMEM),
        scratch_shapes=[pltpu.VMEM((16, 32, 128), F32)] + SQUARE,
        compiler_params=params(),
    )(inside, own, near_links, jump, *near, matrix)


def jumps(table, values, near, out):
    for block in range(16):
        side, far = table[0, block], table[1, block]
        other = jnp.zeros((32, 128), F32)
        for k in range(4):
            other = jnp.where(side == k + 1, near[k][far].astype(F32), other)
        out[block] = jnp.where(table[2, block] > 0, values[block] - other, 0.0)


def diagonal():
    lanes = lax.broadcasted_iota(jnp.int32, (32, 128), 1)
    load = lax.broadcasted_iota(jnp.int32, (32, 128), 0)
    return lanes - load


def own_rows(table, ref):
    return [
        jnp.where(table[6, row] > 0, ref[table[5, row]], 0.0) if ref.shape[0] == 16 else ref[row]
        for row in range(8)
    ]


def product_rows(table, pairs):
    lanes = diagonal()
    rows = [jnp.zeros((32, 128), F32) for _ in range((len(pairs) + 3) // 4)]
    for i, pair in enumerate(pairs):
        left, right = (own_rows(table, ref) for ref in pair)
        total = jnp.zeros((32, 128), F32)
        for one, other in zip(left, right):
            total += one * other
        total = jnp.sum(total, axis=1, keepdims=True)
        rows[i // 4] += jnp.where(lanes == 32 * (i % 4), total, 0.0)
    return [jnp.sum(row, axis=0, keepdims=True) for row in rows]


def by_load(row, count):
    lanes = diagonal()
    return [
        jnp.sum(jnp.where(lanes == 32 * i, row, 0.0), axis=1, keepdims=True) for i in range(count)
    ]


def in_thirds(row):
    index = lax.broadcasted_iota(jnp.int32, (8, 128), 0)
    whole = jnp.zeros((8, 128), F32)
    for i in range(3):
        part = row.astype(BF16).astype(F32)
        whole = jnp.where(index == i, part, whole)
        row = row - part
    return whole


def lane_group():
    return lax.broadcasted_iota(jnp.int32, (8, 128), 1) // 32


def pick(lanes, parts, places):
    out = parts[0]
    for part, place in zip(parts[1:], places[1:]):
        out = jnp.where(lanes == place, part, out)
    return out


def turn(values, groups):
    groups = groups % 4
    return values if groups == 0 else pltpu.roll(values, groups * 32, 1)


def one_hot(columns, first, count):
    listed = jnp.concatenate([columns[first + i : first + i + 1, :] for i in range(count)], axis=1)
    index = lax.broadcasted_iota(jnp.int32, (768, 128 * count), 0)
    return jnp.where(index == listed, 1.0, 0.0).astype(BF16)


def operator_kernel(pairs, table, values, n1, n2, n3, n4, matrix, *refs):
    count = 4 if pairs else 0
    vectors, (w, out, sent), sums, (held, arrived) = (
        refs[:count],
        refs[count : count + 3],
        refs[count + 3 : -2],
        refs[-2:],
    )
    copies = square_copies(matrix, held, arrived)
    jumps(table, values, (n1, n2, n3, n4), w)
    square(w, copies, held, out, sent)
    if pairs:
        r, u, s, d = vectors
        listed = [(r, u), (u, w), (u, s), (d, w)][:pairs]
        sums[0][0] = in_thirds(product_rows(table, listed)[0])


def after_operator(pairs, table, surface, near, matrix, vectors=()):
    outs = (FULL, FULL, SENT) + ((struct((1, 8, 128), F32),) if pairs else ())
    return pl.pallas_call(
        functools.partial(operator_kernel, pairs),
        out_shape=outs,
        in_specs=[SMEM] + [VMEM] * 5 + [ANY] + [VMEM] * len(vectors),
        out_specs=(VMEM,) * len(outs),
        scratch_shapes=SQUARE,
        compiler_params=params(),
    )(table, surface, *near, matrix, *vectors)


def terms_kernel(table, values, n1, n2, n3, n4, coupling, place, extra, jumped, out):
    jumps(table, values, (n1, n2, n3, n4), jumped)
    g = table[4, 0]
    lanes = lane_group()
    terms = []
    for s in range(2):
        got = matmul_t(halves(wide(jumped, s)), coupling[s])
        terms.append((got[:32] + got[32:]).astype(BF16))
    placed = matmul(terms[0], place[:192]) + matmul(terms[1], place[192:])
    at = [lax.rem(g + c, 4) for c in range(4)]
    for block in range(8):
        part = [placed[8 * i : 8 * i + 8, block * 128 : (block + 1) * 128] for i in range(4)]
        turned = [
            turn(pick(lanes, [part[(c + j) % 4] for c in range(4)], at), j) for j in range(4)
        ]
        for c in range(4):
            piece = pick(lanes, [turned[(i - c) % 4] for i in range(4)], at)
            s = block * 4 + c
            more = extra[s if extra.shape[0] > 1 else 0]
            out[pl.ds(s * 64, 64), :] = jnp.concatenate([piece, more] * 4, axis=0).astype(BF16)


def corner_terms(table, surface, near, coupling, place, extra):
    jumped, sent = pl.pallas_call(
        terms_kernel,
        out_shape=(FULL, struct((2048, 128), BF16)),
        in_specs=[SMEM] + [VMEM] * 8,
        out_specs=(VMEM, VMEM),
        compiler_params=params(),
    )(table, surface, *near, coupling, place, extra)
    return jumped, exchange(sent, BOTH)


def source_rows(got, s):
    part = got[pl.ds(s * 64, 64), :].astype(F32)
    return [part[16 * c : 16 * c + 16] for c in range(4)]


def factor_copies(factor, held, arrived, first):
    size = held.shape[1]
    copies = []
    for i in range(4):
        half = first if i < 2 else 1 - first
        at = pl.multiple_of((half * 2 + i % 2) * size, size)
        copies.append(
            pltpu.make_async_copy(factor.at[pl.ds(at, size), :], held.at[i], arrived.at[i])
        )
        copies[-1].start()
    return copies


def core():
    return lax.rem(lax.axis_index("sub"), 2)


def assemble(got, columns):
    lanes = lane_group()
    group = 4
    assembled = jnp.zeros((32, 768), F32)
    for first in range(0, 32, group):
        slots = []
        for s in range(first, first + group):
            part = [rows[:8] for rows in source_rows(got, s)]
            loads = [
                turn(pick(lanes, part, [(i + c) % 4 for c in range(4)]), -i) for i in range(4)
            ]
            slots.append(jnp.concatenate(loads, axis=0).astype(BF16))
        assembled += matmul_t(jnp.concatenate(slots, axis=1), one_hot(columns, first, group))
    return assembled


def forward(assembled, copies, held, away, kept):
    assembled = assembled.astype(BF16)
    chunks = held.shape[1] // 128
    for i in range(4):
        copies[i].wait()
        part = matmul_t(assembled, held[i]).astype(BF16)
        out = away if i < 2 else kept
        for half in range(2):
            for j in range(chunks):
                row = (half * 24 + (i % 2) * chunks + j) * 16
                out[pl.ds(row, 16), :] = part[16 * half : 16 * half + 16, j * 128 : j * 128 + 128]


def first_forward_kernel(
    got, factor, away, home, assembled_u, columns, spilled, held, arrived
):
    copies = factor_copies(factor, held, arrived, 1 - core())
    flag = jnp.zeros((1, 128), F32)
    for s in range(32):
        column = jnp.zeros((1, 128), F32)
        for rows in source_rows(got, s):
            column += rows[8:9] + 256.0 * rows[9:10]
            flag = jnp.maximum(flag, rows[10:11])
        columns[s : s + 1, :] = column.astype(jnp.int32)
    spilled[...] = flag
    assembled_u[...] = assemble(got, columns)
    forward(assembled_u[...], copies, held, away, home)


def next_forward_kernel(first, got, columns, old_u, old_q, old, factor, *refs):
    away, home, assembled_u, assembled_q, kept, held, arrived = refs
    copies = factor_copies(factor, held, arrived, 1 - core())
    total = jnp.zeros((8, 128), F32)
    for s in range(32):
        for rows in source_rows(got, s):
            total += rows[8:]
    gamma, uw, us, dw = by_load(jnp.sum(total, axis=0, keepdims=True), 4)
    if first:
        beta, delta = jnp.zeros_like(gamma), uw
    else:
        beta = gamma / old[0][:, 0:1]
        delta = uw + beta * (us + dw) + beta * beta * old[1][:, 0:1]
    alpha = gamma / delta
    for i, value in enumerate((gamma, delta, alpha, beta)):
        kept[i] = jnp.broadcast_to(value, (32, 128))
    got_q = assemble(got, columns)
    if not first:
        got_q += beta * old_q[...]
    assembled_q[...] = got_q
    assembled_u[...] = old_u[...] - alpha * got_q
    forward(assembled_u[...], copies, held, away, home)


FETCHED = [pltpu.VMEM((4, 1536, 768), BF16), pltpu.SemaphoreType.DMA((4,))]
HALF = struct((768, 128), BF16)
SUMS = struct((32, 768), F32)
KEPT = struct((4, 32, 128), F32)


def first_forward(got, factor):
    return pl.pallas_call(
        first_forward_kernel,
        out_shape=(
            HALF,
            HALF,
            SUMS,
            struct((32, 128), jnp.int32),
            struct((1, 128), F32),
        ),
        in_specs=[VMEM, ANY],
        out_specs=(VMEM,) * 5,
        scratch_shapes=FETCHED,
        compiler_params=params(24),
    )(got, factor)


def next_forward(first, got, columns, old_u, old_q, old, factor):
    return pl.pallas_call(
        functools.partial(next_forward_kernel, first),
        out_shape=(HALF, HALF, SUMS, SUMS, KEPT),
        in_specs=[VMEM] * 5 + [ANY],
        out_specs=(VMEM,) * 5,
        scratch_shapes=FETCHED,
        compiler_params=params(24),
    )(got, columns, old_u, old_q, old, factor)


def pair_kernel(home, got, out):
    out[...] = (home[...].astype(F32) + got[...].astype(F32)).astype(BF16)


def total_kernel(got, out):
    total = got[pl.ds(0, 48), :].astype(F32)
    for peer in range(1, 16):
        total += got[pl.ds(peer * 48, 48), :].astype(F32)
    total = total.astype(BF16)
    for peer in range(16):
        out[pl.ds(peer * 48, 48), :] = total


def coarse_kernel(home, other, factor, columns, out, held, arrived):
    copies = factor_copies(factor, held, arrived, core())
    chunks = held.shape[1] // 128
    solution = jnp.zeros((32, 768), F32)
    for i in range(4):
        got = home if i < 2 else other
        parts = [
            [got[pl.ds((half * 24 + (i % 2) * chunks + j) * 16, 16), :] for j in range(chunks)]
            for half in range(2)
        ]
        rows = jnp.concatenate([jnp.concatenate(part, axis=1) for part in parts], axis=0)
        copies[i].wait()
        solution += matmul(rows, held[i])
    solution = solution.astype(BF16)
    lanes = lane_group()
    for first in range(0, 32, 8):
        picked = matmul(solution, one_hot(columns, first, 8))
        for s in range(8):
            part = [
                turn(picked[8 * i : 8 * i + 8, s * 128 : s * 128 + 128], i) for i in range(4)
            ]
            pieces = [pick(lanes, part, [(i + c) % 4 for i in range(4)]) for c in range(4)]
            out[pl.ds((first + s) * 32, 32), :] = jnp.concatenate(pieces, axis=0).astype(BF16)


def correct_kernel(got, place, coupling, local, out, sent):
    g = lax.axis_index("grp")
    lanes = lane_group()
    at = [lax.rem(g + c, 4) for c in range(4)]
    picked = []
    for block in range(8):
        sums = []
        for c in range(4):
            part = got[pl.ds((block * 4 + c) * 32, 32), :].astype(F32)
            sums.append(part[0:8] + part[8:16] + part[16:24] + part[24:32])
        turned = [
            turn(pick(lanes, [sums[(i - j) % 4] for i in range(4)], at), -j) for j in range(4)
        ]
        loads = [pick(lanes, [turned[(i - c) % 4] for c in range(4)], at) for i in range(4)]
        picked.append(jnp.concatenate(loads, axis=0).astype(BF16))
    picked = jnp.concatenate(picked, axis=1)
    for s in range(2):
        values = matmul_t(picked, place[192 * s : 192 * s + 192]).astype(BF16)
        correction = matmul(values, coupling[s])
        for j in range(8):
            block = local[8 * s + j] + correction[:, 128 * j : 128 * j + 128]
            out[8 * s + j] = block
            sent[8 * s + j] = block.astype(BF16)


def local_kernel(values, matrix, out, held, arrived):
    square(values, square_copies(matrix, held, arrived), held, out)


def local_part(values, matrix):
    return pl.pallas_call(
        local_kernel,
        out_shape=FULL,
        in_specs=[VMEM, ANY],
        out_specs=VMEM,
        scratch_shapes=SQUARE,
        compiler_params=params(),
        cost_estimate=cost(2 * 64 * 2 * 1024 * 1024, 4800000),
    )(values, matrix)


def small_call(kernel, *args):
    return pl.pallas_call(
        kernel,
        out_shape=HALF,
        in_specs=[VMEM] * len(args),
        out_specs=VMEM,
        compiler_params=params(),
    )(*args)


def operate(away, home, local, columns, factor, place, coupling):
    peers = lax.axis_size("sub")
    swap = [(i, i ^ 1) for i in range(peers)]
    kinds = [list(range(first, peers, 2)) for first in range(2)]
    summed = small_call(pair_kernel, home, lax.ppermute(away, "sub", swap))
    got = lax.all_to_all(summed, "sub", 0, 0, axis_index_groups=kinds, tiled=True)
    summed = small_call(total_kernel, got)
    home = lax.all_to_all(summed, "sub", 0, 0, axis_index_groups=kinds, tiled=True)
    coarse = pl.pallas_call(
        coarse_kernel,
        out_shape=struct((1024, 128), BF16),
        in_specs=[VMEM, VMEM, ANY, VMEM],
        out_specs=VMEM,
        scratch_shapes=FETCHED,
        compiler_params=params(24),
    )(home, lax.ppermute(home, "sub", swap), factor, columns)
    got = exchange(coarse, BOTH)
    return pl.pallas_call(
        correct_kernel,
        out_shape=(FULL, SENT),
        in_specs=[VMEM] * 4,
        out_specs=(VMEM, VMEM),
        compiler_params=params(),
    )(got, place, coupling, local)


def first_update_kernel(table, kept, r, u, w, m, x_out, r_out, d_out, s_out, u_out):
    alpha = kept[2]
    own_u, own_w = own_rows(table, u), own_rows(table, w)
    for row in range(8):
        d_out[row] = own_u[row]
        s_out[row] = own_w[row]
        x_out[row] = alpha * own_u[row]
        r_out[row] = r[row] - alpha * own_w[row]
    for b in range(16):
        u_out[b] = u[b] - alpha * m[b]


def update_kernel(
    table, kept, x, r, d, s, u, w, m, q, x_out, r_out, d_out, s_out, u_out, q_out
):
    alpha, beta = kept[2], kept[3]
    own_u, own_w = own_rows(table, u), own_rows(table, w)
    for row in range(8):
        dn = own_u[row] + beta * d[row]
        sn = own_w[row] + beta * s[row]
        d_out[row] = dn
        s_out[row] = sn
        x_out[row] = x[row] + alpha * dn
        r_out[row] = r[row] - alpha * sn
    for b in range(16):
        qn = m[b] + beta * q[b]
        q_out[b] = qn
        u_out[b] = u[b] - alpha * qn


def last_products_kernel(table, values, n1, n2, n3, n4, r, d, s, u, w, q, m, out):
    jumps(table, values, (n1, n2, n3, n4), m)
    pairs = [(r, u), (u, w), (u, s), (d, w), (r, m), (r, q), (w, m), (w, q), (s, m), (s, q)]
    rows = product_rows(table, pairs)
    place = lax.rem(lax.broadcasted_iota(jnp.int32, out.shape, 0), 4)
    whole = jnp.zeros(out.shape, F32)
    for i, row in enumerate(rows):
        whole = jnp.where(place == i, row, whole)
    out[...] = whole


def finish_kernel(table, got, old, x, r, d, s, u, w, m, q, x_out, r_out, d_out):
    place = lax.rem(lax.broadcasted_iota(jnp.int32, got.shape, 0), 4)
    totals = []
    for i in range(3):
        totals += by_load(
            jnp.sum(jnp.where(place == i, got[...], 0.0), axis=0, keepdims=True), 4
        )
    gamma, uw, us, dw, rm, rq, wm, wq, sm, sq = totals[:10]
    beta = gamma / old[0][:, 0:1]
    delta = uw + beta * (us + dw) + beta * beta * old[1][:, 0:1]
    alpha = gamma / delta
    cross = rm + beta * rq + uw + beta * us
    squared = wm + beta * (wq + sm) + beta * beta * sq
    last = (gamma - alpha * cross + alpha * alpha * squared) / gamma
    own_u, own_w, own_m, own_q = (own_rows(table, ref) for ref in (u, w, m, q))
    for row in range(8):
        dn = own_u[row] + beta * d[row]
        x_out[row] = x[row] + alpha * dn
        r_out[row] = r[row] - alpha * (own_w[row] + beta * s[row])
        d_out[row] = own_u[row] - alpha * (own_m[row] + beta * own_q[row]) + last * dn


def fast_path(jump, local_inverse, schur, coupling, factor, own, inside, place, listing):
    table, r, surface, sent = set_up(jump, own, inside, schur)
    u, got = corner_terms(table, surface, from_neighbours(sent), coupling, place, listing)
    away, home, sum_u, columns, spilled = first_forward(got, factor)
    local = local_part(u, local_inverse)
    surface, sent = operate(away, home, local, columns, factor, place, coupling)
    w, surface, sent, sums = after_operator(
        2, table, surface, from_neighbours(sent), schur, (r, u, r, r)
    )
    m, got = corner_terms(table, surface, from_neighbours(sent), coupling, place, sums)
    kept = jnp.zeros(KEPT.shape, F32)
    away, home, sum_u, sum_q, kept = next_forward(True, got, columns, sum_u, sum_u, kept, factor)
    q = m
    x, r, d, s, u = pl.pallas_call(
        first_update_kernel,
        out_shape=(OWN,) * 4 + (FULL,),
        in_specs=[SMEM] + [VMEM] * 5,
        compiler_params=params(),
    )(table, kept, r, u, w, m)
    local = local_part(u, local_inverse)
    surface, sent = operate(away, home, local, columns, factor, place, coupling)
    w, surface, sent, sums = after_operator(
        4, table, surface, from_neighbours(sent), schur, (r, u, s, d)
    )
    m, got = corner_terms(table, surface, from_neighbours(sent), coupling, place, sums)
    away, home, _, _, kept = next_forward(False, got, columns, sum_u, sum_q, kept, factor)
    x, r, d, s, u, q = pl.pallas_call(
        update_kernel,
        out_shape=(OWN,) * 4 + (FULL,) * 2,
        in_specs=[SMEM] + [VMEM] * 9,
        compiler_params=params(),
    )(table, kept, x, r, d, s, u, w, m, q)
    local = local_part(u, local_inverse)
    surface, sent = operate(away, home, local, columns, factor, place, coupling)
    w, surface, sent = after_operator(0, table, surface, from_neighbours(sent), schur)
    m, sums = pl.pallas_call(
        last_products_kernel,
        out_shape=(FULL, struct((512, 128), F32)),
        in_specs=[SMEM] + [VMEM] * 11,
        out_specs=(VMEM, VMEM),
        compiler_params=params(),
    )(table, surface, *from_neighbours(sent), r, d, s, u, w, q)
    got = exchange(sums, BOTH)
    outputs = pl.pallas_call(
        finish_kernel,
        out_shape=(OWN,) * 3,
        in_specs=[SMEM] + [VMEM] * 10,
        compiler_params=params(),
    )(table, got, kept, x, r, d, s, u, w, m, q)
    return jnp.max(spilled) > 0, outputs


def on_device(
    jump_load,
    local_inverse,
    dirichlet_schur,
    corner_coupling,
    corner_map,
    coarse_factor,
    block_links,
    block_counts,
):
    sub_cols = coarse_factor.shape[1]
    n_sub, n_grp = lax.axis_size("sub"), lax.axis_size("grp")
    sub, grp = lax.axis_index("sub"), lax.axis_index("grp")
    flat_map = corner_map.reshape(-1)
    block = flat_map // sub_cols
    column = flat_map - block * sub_cols
    order = jnp.arange(flat_map.shape[0], dtype=jnp.int32)
    before = (block[:, None] == block[None, :]) & (order[None, :] < order[:, None])
    rank = jnp.sum(before.astype(jnp.int32), axis=1)
    slot = block * CAP + rank
    fits = rank < CAP
    lane = (block // 4) * 128 + ((block + grp) % 4) * CAP + rank
    slots = jnp.arange(n_sub * CAP, dtype=jnp.int32)
    place = ((lane[:, None] == slots[None, :]) & fits[:, None]).astype(BF16)
    filled = jnp.where((slot[:, None] == slots[None, :]) & fits[:, None], column[:, None] + 1, 0)
    filled = jnp.sum(filled, axis=0).reshape(n_sub, CAP)
    filled = jnp.where(filled > 0, filled - 1, sub_cols)
    here = (jnp.arange(128, dtype=jnp.int32) // CAP == grp)[None, :]
    spilled = jnp.any(~fits).astype(jnp.int32)
    listing = jnp.stack(
        [
            jnp.where(here, jnp.tile(filled % 256, (1, 4)), 0),
            jnp.where(here, jnp.tile(filled // 256, (1, 4)), 0),
            jnp.broadcast_to(spilled, (n_sub, 128)),
        ],
        axis=1,
    )
    listing = jnp.pad(listing, ((0, 0), (0, 5), (0, 0))).astype(F32)
    alive = jnp.arange(8, dtype=jnp.int32) < block_counts[0]
    own = jnp.concatenate(
        [block_links[0, 0], jnp.where(alive, block_links[0, 1], 0), block_links[0, 2]]
    )
    inside = jnp.stack(
        [sub < n_sub - 1, sub > 0, grp < n_grp - 1, grp > 0, grp.astype(jnp.int32)]
    ).astype(jnp.int32)
    spills, outputs = fast_path(
        jump_load,
        local_inverse,
        dirichlet_schur,
        corner_coupling,
        coarse_factor,
        own,
        inside,
        place,
        listing,
    )
    return lax.cond(
        spills,
        lambda: general_path(
            jump_load,
            local_inverse,
            dirichlet_schur,
            corner_coupling,
            corner_map,
            coarse_factor,
            block_links,
            block_counts,
        ),
        lambda: outputs,
    )


def solution(mesh):
    in_specs = (
        P(("sub", "grp"), None, None),
        P(("sub", "grp"), None, None),
        P(("sub", "grp"), None, None),
        P(("sub", "grp"), None, None),
        P(("sub", "grp"), None),
        P("grp", "sub"),
        P(("sub", "grp"), None, None),
        P(("sub", "grp")),
    )
    out_specs = (
        P(("sub", "grp"), None, None),
        P(("sub", "grp"), None, None),
        P(("sub", "grp"), None, None),
    )
    return jax.shard_map(
        on_device, mesh=mesh, in_specs=in_specs, out_specs=out_specs, check_vma=False
    )
```

```python
import functools

import jax
import jax.numpy as jnp
from jax import lax
from jax.experimental import pallas as pl
from jax.experimental.pallas import tpu as pltpu
from jax.sharding import PartitionSpec as P

NC = 24576
ITERS = 3
CAP = 32
BOTH = ("sub", "grp")
BF16 = jnp.bfloat16
F32 = jnp.float32


NEIGHBOUR_SPOTS = ((2, 1), (0, 1), (1, 2), (1, 0))


def extended(array, sides, width):
    for axis, dim in sides:
        peers, length = (lax.axis_size(axis), array.shape[dim])
        up = [(i, (i + 1) % peers) for i in range(peers - 1)]
        down = [(j, i) for i, j in up]
        last = lax.slice_in_dim(array, length - width, length, axis=dim)
        first = lax.slice_in_dim(array, 0, width, axis=dim)
        before = lax.ppermute(last, axis, up)
        after = lax.ppermute(first, axis, down)
        array = jnp.concatenate([before, array, after], axis=dim)
    return array


def shortened(array):

    def short(part):
        return part.astype(jnp.bfloat16) if part.dtype == jnp.float32 else part

    return jax.tree.map(short, array)


def neighbours(padded):
    return [padded[position[0], position[1]] for position in NEIGHBOUR_SPOTS]


def gather_over_sub(array):
    peers = lax.axis_size("sub")
    every = jnp.broadcast_to(array[None], (peers,) + array.shape)
    every = lax.all_to_all(every, "sub", 0, 0, tiled=True)
    return every.transpose(1, 0, 2).reshape(array.shape[0], -1)


def sum_over_sub(array):
    peers = lax.axis_size("sub")
    parts = array.reshape(array.shape[0], peers, -1).transpose(1, 0, 2)
    parts = lax.all_to_all(parts, "sub", 0, 0, tiled=True)
    return gather_over_sub(jnp.sum(parts.astype(jnp.float32), axis=0).astype(array.dtype))


def general_path(
    jump_load,
    local_inverse,
    dirichlet_schur,
    corner_coupling,
    corner_map,
    coarse_factor,
    block_links,
    block_counts,
):
    capacity = jump_load.shape[0]
    loads = jump_load.shape[1]
    block_width = jump_load.shape[2]
    subdomains = local_inverse.shape[0]
    interface = local_inverse.shape[1]
    per_sub = interface // block_width
    primal = corner_coupling.shape[1]
    sub_cols = coarse_factor.shape[1]
    alive = jnp.arange(capacity, dtype=jnp.int32) < block_counts[0]
    own_blocks = block_links[0, 0]
    heading = jnp.where(alive, block_links[0, 1], 0)
    far_blocks = block_links[0, 2]
    own_weight = alive.astype(jnp.float32)[:, None, None]
    has_far = (heading > 0).astype(jnp.float32)[:, None, None]
    listing = jnp.stack([heading, far_blocks])
    listed = extended(listing[None, None], (("sub", 0), ("grp", 1)), 1)
    facing = jnp.array([2, 1, 4, 3], jnp.int32)
    near_lists = jnp.stack(neighbours(listed))
    in_rows = near_lists[:, 1, :].reshape(-1)
    in_weight = (
        (near_lists[:, 0, :] == facing[:, None]).astype(jnp.float32).reshape(-1)[:, None, None]
    )
    flat_map = corner_map.reshape(-1)

    def spread(values):
        padded = extended(shortened(values[None, None]), (("sub", 0), ("grp", 1)), 1)
        incoming = jnp.concatenate(neighbours(padded), axis=0)
        summed_up = jnp.zeros((subdomains, loads, per_sub, block_width), jnp.float32)
        summed_up = summed_up.at[own_blocks // per_sub, :, own_blocks % per_sub].add(
            values * own_weight
        )
        summed_up = summed_up.at[in_rows // per_sub, :, in_rows % per_sub].add(
            -incoming * in_weight
        )
        return summed_up.reshape(subdomains, loads, interface).astype(jnp.bfloat16)

    def jumps(surface):
        pieces = surface.reshape(subdomains, loads, per_sub, block_width)
        padded = extended(
            pieces[None, None].astype(jnp.bfloat16), (("sub", 0), ("grp", 1)), 1
        ).astype(jnp.float32)
        nearby = jnp.stack([pieces] + neighbours(padded))
        far_values = nearby[heading, far_blocks // per_sub, :, far_blocks % per_sub]
        own_values = pieces[own_blocks // per_sub, :, own_blocks % per_sub]
        return (own_values - far_values * has_far) * own_weight

    def precondition(residual):
        spread_in = spread(residual)
        return jumps(
            jnp.einsum(
                "ski,sij->skj", spread_in, dirichlet_schur, preferred_element_type=jnp.float32
            )
        )

    def column_sum(left, right):
        return jnp.sum(left * right, axis=(0, 2))

    def residual_products(residual, precond):
        return lax.psum(column_sum(residual, precond), ("sub", "grp"))

    residual = jump_load * own_weight
    multipliers = jnp.zeros_like(residual)
    precond = precondition(residual)
    direction = precond
    res_dot = residual_products(residual, precond)
    for iteration in range(ITERS):
        operator_spread_in = spread(direction)
        local_part = jnp.einsum(
            "ski,sij->skj", operator_spread_in, local_inverse, preferred_element_type=jnp.float32
        )
        corner_terms = jnp.einsum(
            "ski,sci->ksc", operator_spread_in, corner_coupling, preferred_element_type=jnp.float32
        )
        scattered = (
            jnp.zeros((loads, NC), jnp.float32)
            .at[:, flat_map]
            .add(corner_terms.reshape(loads, subdomains * primal))
        )
        summed = lax.psum(scattered, ("sub", "grp"))
        assembled = lax.dynamic_slice_in_dim(summed, lax.axis_index("sub") * sub_cols, sub_cols, 1)
        forward_part = lax.dot_general(
            assembled.astype(jnp.bfloat16),
            coarse_factor,
            (((1,), (1,)), ((), ())),
            preferred_element_type=jnp.float32,
        )
        forward = sum_over_sub(forward_part.astype(jnp.bfloat16))
        coarse_part = jnp.dot(forward, coarse_factor, preferred_element_type=jnp.float32)
        coarse = lax.psum(coarse_part.astype(jnp.bfloat16), "grp")
        coarse_all = gather_over_sub(coarse)
        picked = coarse_all[:, flat_map].reshape(loads, subdomains, primal)
        correction = jnp.einsum(
            "ksc,sci->ski", picked, corner_coupling, preferred_element_type=jnp.float32
        )
        applied = jumps(local_part + correction)
        curvature = lax.psum(column_sum(direction, applied), ("sub", "grp"))
        step_size = res_dot / curvature
        multipliers = multipliers + step_size[None, :, None] * direction
        residual = residual - step_size[None, :, None] * applied
        precond = precondition(residual)
        new_dot = residual_products(residual, precond)
        direction = precond + (new_dot / res_dot)[None, :, None] * direction
        res_dot = new_dot
    return (multipliers, residual, direction)


def struct(shape, dtype):
    return jax.ShapeDtypeStruct(shape, dtype)


def cost(flops, size):
    return pl.CostEstimate(flops=flops, bytes_accessed=size, transcendentals=0)


def params(mib=16):
    return pltpu.CompilerParams(vmem_limit_bytes=mib * 1024 * 1024)


SMEM = pl.BlockSpec(memory_space=pltpu.SMEM)
VMEM = pl.BlockSpec(memory_space=pltpu.VMEM)
ANY = pl.BlockSpec(memory_space=pl.ANY)


def matmul(left, right):
    return lax.dot_general(left, right, (((1,), (0,)), ((), ())), preferred_element_type=F32)


def matmul_t(left, right):
    return lax.dot_general(left, right, (((1,), (1,)), ((), ())), preferred_element_type=F32)


def partners(axis, first):
    peers = lax.axis_size(axis)
    return [(i, (((i + first) ^ 1) - first) % peers) for i in range(peers)]


def from_neighbours(array):
    return [
        lax.ppermute(array, axis, partners(axis, first))
        for axis, first in (("grp", 0), ("grp", 1), ("sub", 1), ("sub", 0))
    ]


def buffers(sub, grp):
    odd_sub, odd_grp = sub % 2, grp % 2
    sides = [3 + odd_grp, 4 - odd_grp, 2 - odd_sub, 1 + odd_sub]
    places = [4 - odd_sub, 3 + odd_sub, 1 + odd_grp, 2 - odd_grp]
    return sides + places


def exchange(array, axes):
    return lax.all_to_all(array, axes, 0, 0, tiled=True)


def halves(values):
    high = values.astype(BF16)
    return jnp.concatenate([high, (values - high.astype(F32)).astype(BF16)], axis=0)


def wide(ref, subdomain):
    return jnp.concatenate([ref[subdomain * 8 + j] for j in range(8)], axis=1)


def square_copies(matrix, held, arrived):
    copies = [pltpu.make_async_copy(matrix.at[s], held.at[s], arrived.at[s]) for s in range(2)]
    for copy in copies:
        copy.start()
    return copies


def square(values, copies, held, out, sent=None):
    for s in range(2):
        full = halves(wide(values, s))
        copies[s].wait()
        got = matmul(full, held[s])
        got = got[:32] + got[32:]
        for j in range(8):
            block = got[:, j * 128 : j * 128 + 128]
            out[8 * s + j] = block
            if sent is not None:
                sent[8 * s + j] = block.astype(BF16)


SQUARE = [pltpu.VMEM((2, 1024, 1024), BF16), pltpu.SemaphoreType.DMA((2,))]
FULL = struct((16, 32, 128), F32)
OWN = struct((8, 32, 128), F32)
SENT = struct((16, 32, 128), BF16)


def first_kernel(
    inside, own, near, jump, near1, near2, near3, near4, matrix, table, r, out, sent, first, held, arrived
):
    copies = square_copies(matrix, held, arrived)
    for block in range(16):
        for row in range(4):
            table[row, block] = 0
        table[4, block] = inside[4]
        table[5, block] = own[block % 8]
        table[6, block] = (own[8 + block % 8] > 0).astype(jnp.int32)
    first[...] = jnp.zeros_like(first)
    r[...] = jnp.zeros_like(r)
    for m in range(8):
        block = own[m]

        @pl.when(own[8 + m] > 0)
        def _():
            side = own[8 + m]
            table[0, block] = jnp.where(inside[side - 1] > 0, inside[8 + side], 0)
            table[1, block] = own[16 + m]
            table[2, block] = 1
            table[3, block] = 1
            first[block] = jump[m]
            r[m] = jump[m]

    for k, rows in enumerate((near1, near2, near3, near4)):
        side = inside[5 + k]
        facing = jnp.where(lax.rem(side, 2) == 1, side + 1, side - 1)
        for m in range(8):

            @pl.when((inside[side - 1] > 0) & (near[k, 8 + m] == facing))
            def _():
                block = near[k, 16 + m]
                table[0, block] = k + 1
                table[1, block] = near[k, m]
                table[2, block] = 1
                first[block] = -rows[pl.ds(m * 32, 32), :]

    square(first, copies, held, out, sent)


def set_up(jump, own, inside, matrix):
    rows = jnp.concatenate(
        [jump.reshape(256, 128), jnp.pad(own.astype(F32)[None, :], ((0, 7), (0, 104)))], axis=0
    )
    near = from_neighbours(rows)
    near_links = jnp.stack([n[256, :24] for n in near]).astype(jnp.int32)
    return pl.pallas_call(
        first_kernel,
        out_shape=(struct((7, 16), jnp.int32), OWN, FULL, SENT),
        in_specs=[SMEM, SMEM, SMEM] + [VMEM] * 5 + [ANY],
        out_specs=(SMEM, VMEM, VMEM, VMEM),
        scratch_shapes=[pltpu.VMEM((16, 32, 128), F32)] + SQUARE,
        compiler_params=params(),
    )(inside, own, near_links, jump, *near, matrix)


def jumps(table, values, near, out):
    for block in range(16):
        side, far = table[0, block], table[1, block]
        other = jnp.zeros((32, 128), F32)
        for k in range(4):
            other = jnp.where(side == k + 1, near[k][far].astype(F32), other)
        out[block] = jnp.where(table[2, block] > 0, values[block] - other, 0.0)


def diagonal():
    lanes = lax.broadcasted_iota(jnp.int32, (32, 128), 1)
    load = lax.broadcasted_iota(jnp.int32, (32, 128), 0)
    return lanes - load


def own_rows(table, ref):
    return [
        jnp.where(table[6, row] > 0, ref[table[5, row]], 0.0) if ref.shape[0] == 16 else ref[row]
        for row in range(8)
    ]


def product_rows(table, pairs):
    lanes = diagonal()
    rows = [jnp.zeros((32, 128), F32) for _ in range((len(pairs) + 3) // 4)]
    for i, pair in enumerate(pairs):
        left, right = (own_rows(table, ref) for ref in pair)
        total = jnp.zeros((32, 128), F32)
        for one, other in zip(left, right):
            total += one * other
        total = jnp.sum(total, axis=1, keepdims=True)
        rows[i // 4] += jnp.where(lanes == 32 * (i % 4), total, 0.0)
    return [jnp.sum(row, axis=0, keepdims=True) for row in rows]


def by_load(row, count):
    lanes = diagonal()
    return [
        jnp.sum(jnp.where(lanes == 32 * i, row, 0.0), axis=1, keepdims=True) for i in range(count)
    ]


def in_thirds(row):
    index = lax.broadcasted_iota(jnp.int32, (8, 128), 0)
    whole = jnp.zeros((8, 128), F32)
    for i in range(3):
        part = row.astype(BF16).astype(F32)
        whole = jnp.where(index == i, part, whole)
        row = row - part
    return whole


def lane_group():
    return lax.broadcasted_iota(jnp.int32, (8, 128), 1) // 32


def pick(lanes, parts, places):
    out = parts[0]
    for part, place in zip(parts[1:], places[1:]):
        out = jnp.where(lanes == place, part, out)
    return out


def turn(values, groups):
    groups = groups % 4
    return values if groups == 0 else pltpu.roll(values, groups * 32, 1)


def one_hot(columns, first, count):
    listed = jnp.concatenate([columns[first + i : first + i + 1, :] for i in range(count)], axis=1)
    index = lax.broadcasted_iota(jnp.int32, (768, 128 * count), 0)
    return jnp.where(index == listed, 1.0, 0.0).astype(BF16)


def operator_kernel(pairs, table, values, n1, n2, n3, n4, matrix, *refs):
    count = 4 if pairs else 0
    vectors, (w, out, sent), sums, (held, arrived) = (
        refs[:count],
        refs[count : count + 3],
        refs[count + 3 : -2],
        refs[-2:],
    )
    copies = square_copies(matrix, held, arrived)
    jumps(table, values, (n1, n2, n3, n4), w)
    if pairs:
        r, u, s, d = vectors
        listed = [(r, u), (u, w), (u, s), (d, w)][:pairs]
        sums[0][0] = in_thirds(product_rows(table, listed)[0])
    square(w, copies, held, out, sent)


def after_operator(pairs, table, surface, near, matrix, vectors=()):
    outs = (FULL, FULL, SENT) + ((struct((1, 8, 128), F32),) if pairs else ())
    return pl.pallas_call(
        functools.partial(operator_kernel, pairs),
        out_shape=outs,
        in_specs=[SMEM] + [VMEM] * 5 + [ANY] + [VMEM] * len(vectors),
        out_specs=(VMEM,) * len(outs),
        scratch_shapes=SQUARE,
        compiler_params=params(),
    )(table, surface, *near, matrix, *vectors)


def terms_kernel(table, values, n1, n2, n3, n4, coupling, place, extra, jumped, out):
    jumps(table, values, (n1, n2, n3, n4), jumped)
    g = table[4, 0]
    lanes = lane_group()
    terms = []
    for s in range(2):
        got = matmul_t(halves(wide(jumped, s)), coupling[s])
        terms.append((got[:32] + got[32:]).astype(BF16))
    placed = matmul(terms[0], place[:192]) + matmul(terms[1], place[192:])
    at = [lax.rem(g + c, 4) for c in range(4)]
    for block in range(8):
        part = [placed[8 * i : 8 * i + 8, block * 128 : (block + 1) * 128] for i in range(4)]
        turned = [
            turn(pick(lanes, [part[(c + j) % 4] for c in range(4)], at), j) for j in range(4)
        ]
        for c in range(4):
            piece = pick(lanes, [turned[(i - c) % 4] for i in range(4)], at)
            s = block * 4 + c
            more = extra[s if extra.shape[0] > 1 else 0]
            out[pl.ds(s * 64, 64), :] = jnp.concatenate([piece, more] * 4, axis=0).astype(BF16)


def corner_terms(table, surface, near, coupling, place, extra):
    jumped, sent = pl.pallas_call(
        terms_kernel,
        out_shape=(FULL, struct((2048, 128), BF16)),
        in_specs=[SMEM] + [VMEM] * 8,
        out_specs=(VMEM, VMEM),
        compiler_params=params(),
    )(table, surface, *near, coupling, place, extra)
    return jumped, exchange(sent, BOTH)


def source_rows(got, s):
    part = got[pl.ds(s * 64, 64), :].astype(F32)
    return [part[16 * c : 16 * c + 16] for c in range(4)]


def factor_copies(factor, held, arrived, half):
    size = held.shape[1]
    copies = []
    for i in range(2):
        at = pl.multiple_of((half * 2 + i) * size, size)
        copies.append(
            pltpu.make_async_copy(factor.at[pl.ds(at, size), :], held.at[i], arrived.at[i])
        )
        copies[-1].start()
    return copies


def core():
    return lax.rem(lax.axis_index("sub"), 2)


def assemble(got, columns):
    lanes = lane_group()
    group = 4
    assembled = jnp.zeros((32, 768), F32)
    for first in range(0, 32, group):
        slots = []
        for s in range(first, first + group):
            part = [rows[:8] for rows in source_rows(got, s)]
            loads = [
                turn(pick(lanes, part, [(i + c) % 4 for c in range(4)]), -i) for i in range(4)
            ]
            slots.append(jnp.concatenate(loads, axis=0).astype(BF16))
        assembled += matmul_t(jnp.concatenate(slots, axis=1), one_hot(columns, first, group))
    return assembled


def forward(assembled, copies, held, out):
    assembled = assembled.astype(BF16)
    chunks = held.shape[1] // 128
    for i in range(2):
        copies[i].wait()
        part = matmul_t(assembled, held[i]).astype(BF16)
        for half in range(2):
            for j in range(chunks):
                row = (half * 24 + i * chunks + j) * 16
                out[pl.ds(row, 16), :] = part[16 * half : 16 * half + 16, j * 128 : j * 128 + 128]


def home_kernel(assembled, factor, out, held, arrived):
    forward(assembled[...], factor_copies(factor, held, arrived, core()), held, out)


def home_forward(assembled, factor):
    return pl.pallas_call(
        home_kernel,
        out_shape=HALF,
        in_specs=[VMEM, ANY],
        out_specs=VMEM,
        scratch_shapes=FETCHED,
        compiler_params=params(),
        cost_estimate=cost(2 * 32 * 768 * 3072, 5000000),
    )(assembled, factor)


def first_forward_kernel(
    got, factor, away, assembled_u, columns, spilled, held, arrived
):
    copies = factor_copies(factor, held, arrived, 1 - core())
    flag = jnp.zeros((1, 128), F32)
    for s in range(32):
        column = jnp.zeros((1, 128), F32)
        for rows in source_rows(got, s):
            column += rows[8:9] + 256.0 * rows[9:10]
            flag = jnp.maximum(flag, rows[10:11])
        columns[s : s + 1, :] = column.astype(jnp.int32)
    spilled[...] = flag
    assembled_u[...] = assemble(got, columns)
    forward(assembled_u[...], copies, held, away)


def next_forward_kernel(first, got, columns, old_u, old_q, old, factor, *refs):
    away, assembled_u, assembled_q, kept, held, arrived = refs
    copies = factor_copies(factor, held, arrived, 1 - core())
    total = jnp.zeros((8, 128), F32)
    for s in range(32):
        for rows in source_rows(got, s):
            total += rows[8:]
    gamma, uw, us, dw = by_load(jnp.sum(total, axis=0, keepdims=True), 4)
    if first:
        beta, delta = jnp.zeros_like(gamma), uw
    else:
        beta = gamma / old[0][:, 0:1]
        delta = uw + beta * (us + dw) + beta * beta * old[1][:, 0:1]
    alpha = gamma / delta
    for i, value in enumerate((gamma, delta, alpha, beta)):
        kept[i] = jnp.broadcast_to(value, (32, 128))
    got_q = assemble(got, columns)
    if not first:
        got_q += beta * old_q[...]
    assembled_q[...] = got_q
    assembled_u[...] = old_u[...] - alpha * got_q
    forward(assembled_u[...], copies, held, away)


FETCHED = [pltpu.VMEM((2, 1536, 768), BF16), pltpu.SemaphoreType.DMA((2,))]
HALF = struct((768, 128), BF16)
SUMS = struct((32, 768), F32)
KEPT = struct((4, 32, 128), F32)


def first_forward(got, factor):
    return pl.pallas_call(
        first_forward_kernel,
        out_shape=(
            HALF,
            SUMS,
            struct((32, 128), jnp.int32),
            struct((1, 128), F32),
        ),
        in_specs=[VMEM, ANY],
        out_specs=(VMEM,) * 4,
        scratch_shapes=FETCHED,
        compiler_params=params(24),
    )(got, factor)


def next_forward(first, got, columns, old_u, old_q, old, factor):
    return pl.pallas_call(
        functools.partial(next_forward_kernel, first),
        out_shape=(HALF, SUMS, SUMS, KEPT),
        in_specs=[VMEM] * 5 + [ANY],
        out_specs=(VMEM,) * 4,
        scratch_shapes=FETCHED,
        compiler_params=params(24),
    )(got, columns, old_u, old_q, old, factor)


def pair_kernel(home, got, out):
    out[...] = (home[...].astype(F32) + got[...].astype(F32)).astype(BF16)


def total_kernel(got, out):
    total = got[pl.ds(0, 48), :].astype(F32)
    for peer in range(1, 16):
        total += got[pl.ds(peer * 48, 48), :].astype(F32)
    total = total.astype(BF16)
    for peer in range(16):
        out[pl.ds(peer * 48, 48), :] = total


def coarse_half(got, copies, held):
    chunks = held.shape[1] // 128
    solution = jnp.zeros((32, 768), F32)
    for i in range(2):
        parts = [
            [got[pl.ds((half * 24 + i * chunks + j) * 16, 16), :] for j in range(chunks)]
            for half in range(2)
        ]
        rows = jnp.concatenate([jnp.concatenate(part, axis=1) for part in parts], axis=0)
        copies[i].wait()
        solution += matmul(rows, held[i])
    return solution


def home_coarse_kernel(got, factor, out, held, arrived):
    out[...] = coarse_half(got, factor_copies(factor, held, arrived, core()), held)


def coarse_kernel(got, begun, factor, columns, out, held, arrived):
    copies = factor_copies(factor, held, arrived, 1 - core())
    solution = begun[...] + coarse_half(got, copies, held)
    solution = solution.astype(BF16)
    lanes = lane_group()
    for first in range(0, 32, 8):
        picked = matmul(solution, one_hot(columns, first, 8))
        for s in range(8):
            part = [
                turn(picked[8 * i : 8 * i + 8, s * 128 : s * 128 + 128], i) for i in range(4)
            ]
            pieces = [pick(lanes, part, [(i + c) % 4 for i in range(4)]) for c in range(4)]
            out[pl.ds((first + s) * 32, 32), :] = jnp.concatenate(pieces, axis=0).astype(BF16)


def correct_kernel(got, place, coupling, local, out, sent):
    g = lax.axis_index("grp")
    lanes = lane_group()
    at = [lax.rem(g + c, 4) for c in range(4)]
    picked = []
    for block in range(8):
        sums = []
        for c in range(4):
            part = got[pl.ds((block * 4 + c) * 32, 32), :].astype(F32)
            sums.append(part[0:8] + part[8:16] + part[16:24] + part[24:32])
        turned = [
            turn(pick(lanes, [sums[(i - j) % 4] for i in range(4)], at), -j) for j in range(4)
        ]
        loads = [pick(lanes, [turned[(i - c) % 4] for c in range(4)], at) for i in range(4)]
        picked.append(jnp.concatenate(loads, axis=0).astype(BF16))
    picked = jnp.concatenate(picked, axis=1)
    for s in range(2):
        values = matmul_t(picked, place[192 * s : 192 * s + 192]).astype(BF16)
        correction = matmul(values, coupling[s])
        for j in range(8):
            block = local[8 * s + j] + correction[:, 128 * j : 128 * j + 128]
            out[8 * s + j] = block
            sent[8 * s + j] = block.astype(BF16)


def local_kernel(values, matrix, out, held, arrived):
    square(values, square_copies(matrix, held, arrived), held, out)


def local_part(values, matrix):
    return pl.pallas_call(
        local_kernel,
        out_shape=FULL,
        in_specs=[VMEM, ANY],
        out_specs=VMEM,
        scratch_shapes=SQUARE,
        compiler_params=params(),
        cost_estimate=cost(2 * 64 * 2 * 1024 * 1024, 4800000),
    )(values, matrix)


def small_call(kernel, *args):
    return pl.pallas_call(
        kernel,
        out_shape=HALF,
        in_specs=[VMEM] * len(args),
        out_specs=VMEM,
        compiler_params=params(),
    )(*args)


def operate(away, sums, local, columns, factor, place, coupling):
    peers = lax.axis_size("sub")
    swap = partners("sub", 0)
    kinds = [list(range(first, peers, 2)) for first in range(2)]
    got = lax.ppermute(away, "sub", swap)
    summed = small_call(pair_kernel, home_forward(sums, factor), got)
    got = lax.all_to_all(summed, "sub", 0, 0, axis_index_groups=kinds, tiled=True)
    summed = small_call(total_kernel, got)
    home = lax.all_to_all(summed, "sub", 0, 0, axis_index_groups=kinds, tiled=True)
    other = lax.ppermute(home, "sub", swap)
    begun = pl.pallas_call(
        home_coarse_kernel,
        out_shape=SUMS,
        in_specs=[VMEM, ANY],
        out_specs=VMEM,
        scratch_shapes=FETCHED,
        compiler_params=params(),
        cost_estimate=cost(2 * 32 * 768 * 3072, 5000000),
    )(home, factor)
    coarse = pl.pallas_call(
        coarse_kernel,
        out_shape=struct((1024, 128), BF16),
        in_specs=[VMEM, VMEM, ANY, VMEM],
        out_specs=VMEM,
        scratch_shapes=FETCHED,
        compiler_params=params(24),
    )(other, begun, factor, columns)
    got = exchange(coarse, BOTH)
    return pl.pallas_call(
        correct_kernel,
        out_shape=(FULL, SENT),
        in_specs=[VMEM] * 4,
        out_specs=(VMEM, VMEM),
        compiler_params=params(),
    )(got, place, coupling, local)


def first_update_kernel(table, kept, r, u, w, m, x_out, r_out, d_out, s_out, u_out):
    alpha = kept[2]
    own_u, own_w = own_rows(table, u), own_rows(table, w)
    for row in range(8):
        d_out[row] = own_u[row]
        s_out[row] = own_w[row]
        x_out[row] = alpha * own_u[row]
        r_out[row] = r[row] - alpha * own_w[row]
    for b in range(16):
        u_out[b] = u[b] - alpha * m[b]


def update_kernel(
    table, kept, x, r, d, s, u, w, m, q, x_out, r_out, d_out, s_out, u_out, q_out
):
    alpha, beta = kept[2], kept[3]
    own_u, own_w = own_rows(table, u), own_rows(table, w)
    for row in range(8):
        dn = own_u[row] + beta * d[row]
        sn = own_w[row] + beta * s[row]
        d_out[row] = dn
        s_out[row] = sn
        x_out[row] = x[row] + alpha * dn
        r_out[row] = r[row] - alpha * sn
    for b in range(16):
        qn = m[b] + beta * q[b]
        q_out[b] = qn
        u_out[b] = u[b] - alpha * qn


def last_products_kernel(table, values, n1, n2, n3, n4, r, d, s, u, w, q, m, out):
    jumps(table, values, (n1, n2, n3, n4), m)
    pairs = [(r, u), (u, w), (u, s), (d, w), (r, m), (r, q), (w, m), (w, q), (s, m), (s, q)]
    rows = product_rows(table, pairs)
    place = lax.rem(lax.broadcasted_iota(jnp.int32, out.shape, 0), 4)
    whole = jnp.zeros(out.shape, F32)
    for i, row in enumerate(rows):
        whole = jnp.where(place == i, row, whole)
    out[...] = whole


def finish_kernel(table, got, old, x, r, d, s, u, w, m, q, x_out, r_out, d_out):
    place = lax.rem(lax.broadcasted_iota(jnp.int32, got.shape, 0), 4)
    totals = []
    for i in range(3):
        totals += by_load(
            jnp.sum(jnp.where(place == i, got[...], 0.0), axis=0, keepdims=True), 4
        )
    gamma, uw, us, dw, rm, rq, wm, wq, sm, sq = totals[:10]
    beta = gamma / old[0][:, 0:1]
    delta = uw + beta * (us + dw) + beta * beta * old[1][:, 0:1]
    alpha = gamma / delta
    cross = rm + beta * rq + uw + beta * us
    squared = wm + beta * (wq + sm) + beta * beta * sq
    last = (gamma - alpha * cross + alpha * alpha * squared) / gamma
    own_u, own_w, own_m, own_q = (own_rows(table, ref) for ref in (u, w, m, q))
    for row in range(8):
        dn = own_u[row] + beta * d[row]
        x_out[row] = x[row] + alpha * dn
        r_out[row] = r[row] - alpha * (own_w[row] + beta * s[row])
        d_out[row] = own_u[row] - alpha * (own_m[row] + beta * own_q[row]) + last * dn


def fast_path(jump, local_inverse, schur, coupling, factor, own, inside, place, listing):
    table, r, surface, sent = set_up(jump, own, inside, schur)
    u, got = corner_terms(table, surface, from_neighbours(sent), coupling, place, listing)
    away, sum_u, columns, spilled = first_forward(got, factor)
    local = local_part(u, local_inverse)
    surface, sent = operate(away, sum_u, local, columns, factor, place, coupling)
    w, surface, sent, sums = after_operator(
        2, table, surface, from_neighbours(sent), schur, (r, u, r, r)
    )
    m, got = corner_terms(table, surface, from_neighbours(sent), coupling, place, sums)
    kept = jnp.zeros(KEPT.shape, F32)
    away, sum_u, sum_q, kept = next_forward(True, got, columns, sum_u, sum_u, kept, factor)
    q = m
    x, r, d, s, u = pl.pallas_call(
        first_update_kernel,
        out_shape=(OWN,) * 4 + (FULL,),
        in_specs=[SMEM] + [VMEM] * 5,
        compiler_params=params(),
    )(table, kept, r, u, w, m)
    local = local_part(u, local_inverse)
    surface, sent = operate(away, sum_u, local, columns, factor, place, coupling)
    w, surface, sent, sums = after_operator(
        4, table, surface, from_neighbours(sent), schur, (r, u, s, d)
    )
    m, got = corner_terms(table, surface, from_neighbours(sent), coupling, place, sums)
    away, sum_u, _, kept = next_forward(False, got, columns, sum_u, sum_q, kept, factor)
    x, r, d, s, u, q = pl.pallas_call(
        update_kernel,
        out_shape=(OWN,) * 4 + (FULL,) * 2,
        in_specs=[SMEM] + [VMEM] * 9,
        compiler_params=params(),
    )(table, kept, x, r, d, s, u, w, m, q)
    local = local_part(u, local_inverse)
    surface, sent = operate(away, sum_u, local, columns, factor, place, coupling)
    w, surface, sent = after_operator(0, table, surface, from_neighbours(sent), schur)
    m, sums = pl.pallas_call(
        last_products_kernel,
        out_shape=(FULL, struct((512, 128), F32)),
        in_specs=[SMEM] + [VMEM] * 11,
        out_specs=(VMEM, VMEM),
        compiler_params=params(),
    )(table, surface, *from_neighbours(sent), r, d, s, u, w, q)
    got = exchange(sums, BOTH)
    outputs = pl.pallas_call(
        finish_kernel,
        out_shape=(OWN,) * 3,
        in_specs=[SMEM] + [VMEM] * 10,
        compiler_params=params(),
    )(table, got, kept, x, r, d, s, u, w, m, q)
    return jnp.max(spilled) > 0, outputs


def on_device(
    jump_load,
    local_inverse,
    dirichlet_schur,
    corner_coupling,
    corner_map,
    coarse_factor,
    block_links,
    block_counts,
):
    sub_cols = coarse_factor.shape[1]
    n_sub, n_grp = lax.axis_size("sub"), lax.axis_size("grp")
    sub, grp = lax.axis_index("sub"), lax.axis_index("grp")
    flat_map = corner_map.reshape(-1)
    block = flat_map // sub_cols
    column = flat_map - block * sub_cols
    order = jnp.arange(flat_map.shape[0], dtype=jnp.int32)
    before = (block[:, None] == block[None, :]) & (order[None, :] < order[:, None])
    rank = jnp.sum(before.astype(jnp.int32), axis=1)
    slot = block * CAP + rank
    fits = rank < CAP
    lane = (block // 4) * 128 + ((block + grp) % 4) * CAP + rank
    slots = jnp.arange(n_sub * CAP, dtype=jnp.int32)
    place = ((lane[:, None] == slots[None, :]) & fits[:, None]).astype(BF16)
    filled = jnp.where((slot[:, None] == slots[None, :]) & fits[:, None], column[:, None] + 1, 0)
    filled = jnp.sum(filled, axis=0).reshape(n_sub, CAP)
    filled = jnp.where(filled > 0, filled - 1, sub_cols)
    here = (jnp.arange(128, dtype=jnp.int32) // CAP == grp)[None, :]
    spilled = jnp.any(~fits).astype(jnp.int32)
    listing = jnp.stack(
        [
            jnp.where(here, jnp.tile(filled % 256, (1, 4)), 0),
            jnp.where(here, jnp.tile(filled // 256, (1, 4)), 0),
            jnp.broadcast_to(spilled, (n_sub, 128)),
        ],
        axis=1,
    )
    listing = jnp.pad(listing, ((0, 0), (0, 5), (0, 0))).astype(F32)
    alive = jnp.arange(8, dtype=jnp.int32) < block_counts[0]
    own = jnp.concatenate(
        [block_links[0, 0], jnp.where(alive, block_links[0, 1], 0), block_links[0, 2]]
    )
    inside = jnp.stack(
        [sub < n_sub - 1, sub > 0, grp < n_grp - 1, grp > 0, grp] + buffers(sub, grp)
    ).astype(jnp.int32)
    spills, outputs = fast_path(
        jump_load,
        local_inverse,
        dirichlet_schur,
        corner_coupling,
        coarse_factor,
        own,
        inside,
        place,
        listing,
    )
    return lax.cond(
        spills,
        lambda: general_path(
            jump_load,
            local_inverse,
            dirichlet_schur,
            corner_coupling,
            corner_map,
            coarse_factor,
            block_links,
            block_counts,
        ),
        lambda: outputs,
    )


def solution(mesh):
    in_specs = (
        P(("sub", "grp"), None, None),
        P(("sub", "grp"), None, None),
        P(("sub", "grp"), None, None),
        P(("sub", "grp"), None, None),
        P(("sub", "grp"), None),
        P("grp", "sub"),
        P(("sub", "grp"), None, None),
        P(("sub", "grp")),
    )
    out_specs = (
        P(("sub", "grp"), None, None),
        P(("sub", "grp"), None, None),
        P(("sub", "grp"), None, None),
    )
    return jax.shard_map(
        on_device, mesh=mesh, in_specs=in_specs, out_specs=out_specs, check_vma=False
    )
```

```python
import functools

import jax
import jax.numpy as jnp
from jax import lax
from jax.experimental import pallas as pl
from jax.experimental.pallas import tpu as pltpu
from jax.sharding import PartitionSpec as P

NC = 24576
ITERS = 3
CAP = 32
BOTH = ("sub", "grp")
BF16 = jnp.bfloat16
F32 = jnp.float32


NEIGHBOUR_SPOTS = ((2, 1), (0, 1), (1, 2), (1, 0))


def extended(array, sides, width):
    for axis, dim in sides:
        peers, length = (lax.axis_size(axis), array.shape[dim])
        up = [(i, (i + 1) % peers) for i in range(peers - 1)]
        down = [(j, i) for i, j in up]
        last = lax.slice_in_dim(array, length - width, length, axis=dim)
        first = lax.slice_in_dim(array, 0, width, axis=dim)
        before = lax.ppermute(last, axis, up)
        after = lax.ppermute(first, axis, down)
        array = jnp.concatenate([before, array, after], axis=dim)
    return array


def shortened(array):

    def short(part):
        return part.astype(jnp.bfloat16) if part.dtype == jnp.float32 else part

    return jax.tree.map(short, array)


def neighbours(padded):
    return [padded[position[0], position[1]] for position in NEIGHBOUR_SPOTS]


def gather_over_sub(array):
    peers = lax.axis_size("sub")
    every = jnp.broadcast_to(array[None], (peers,) + array.shape)
    every = lax.all_to_all(every, "sub", 0, 0, tiled=True)
    return every.transpose(1, 0, 2).reshape(array.shape[0], -1)


def sum_over_sub(array):
    peers = lax.axis_size("sub")
    parts = array.reshape(array.shape[0], peers, -1).transpose(1, 0, 2)
    parts = lax.all_to_all(parts, "sub", 0, 0, tiled=True)
    return gather_over_sub(jnp.sum(parts.astype(jnp.float32), axis=0).astype(array.dtype))


def general_path(
    jump_load,
    local_inverse,
    dirichlet_schur,
    corner_coupling,
    corner_map,
    coarse_factor,
    block_links,
    block_counts,
):
    capacity = jump_load.shape[0]
    loads = jump_load.shape[1]
    block_width = jump_load.shape[2]
    subdomains = local_inverse.shape[0]
    interface = local_inverse.shape[1]
    per_sub = interface // block_width
    primal = corner_coupling.shape[1]
    sub_cols = coarse_factor.shape[1]
    alive = jnp.arange(capacity, dtype=jnp.int32) < block_counts[0]
    own_blocks = block_links[0, 0]
    heading = jnp.where(alive, block_links[0, 1], 0)
    far_blocks = block_links[0, 2]
    own_weight = alive.astype(jnp.float32)[:, None, None]
    has_far = (heading > 0).astype(jnp.float32)[:, None, None]
    listing = jnp.stack([heading, far_blocks])
    listed = extended(listing[None, None], (("sub", 0), ("grp", 1)), 1)
    facing = jnp.array([2, 1, 4, 3], jnp.int32)
    near_lists = jnp.stack(neighbours(listed))
    in_rows = near_lists[:, 1, :].reshape(-1)
    in_weight = (
        (near_lists[:, 0, :] == facing[:, None]).astype(jnp.float32).reshape(-1)[:, None, None]
    )
    flat_map = corner_map.reshape(-1)

    def spread(values):
        padded = extended(shortened(values[None, None]), (("sub", 0), ("grp", 1)), 1)
        incoming = jnp.concatenate(neighbours(padded), axis=0)
        summed_up = jnp.zeros((subdomains, loads, per_sub, block_width), jnp.float32)
        summed_up = summed_up.at[own_blocks // per_sub, :, own_blocks % per_sub].add(
            values * own_weight
        )
        summed_up = summed_up.at[in_rows // per_sub, :, in_rows % per_sub].add(
            -incoming * in_weight
        )
        return summed_up.reshape(subdomains, loads, interface).astype(jnp.bfloat16)

    def jumps(surface):
        pieces = surface.reshape(subdomains, loads, per_sub, block_width)
        padded = extended(
            pieces[None, None].astype(jnp.bfloat16), (("sub", 0), ("grp", 1)), 1
        ).astype(jnp.float32)
        nearby = jnp.stack([pieces] + neighbours(padded))
        far_values = nearby[heading, far_blocks // per_sub, :, far_blocks % per_sub]
        own_values = pieces[own_blocks // per_sub, :, own_blocks % per_sub]
        return (own_values - far_values * has_far) * own_weight

    def precondition(residual):
        spread_in = spread(residual)
        return jumps(
            jnp.einsum(
                "ski,sij->skj", spread_in, dirichlet_schur, preferred_element_type=jnp.float32
            )
        )

    def column_sum(left, right):
        return jnp.sum(left * right, axis=(0, 2))

    def residual_products(residual, precond):
        return lax.psum(column_sum(residual, precond), ("sub", "grp"))

    residual = jump_load * own_weight
    multipliers = jnp.zeros_like(residual)
    precond = precondition(residual)
    direction = precond
    res_dot = residual_products(residual, precond)
    for iteration in range(ITERS):
        operator_spread_in = spread(direction)
        local_part = jnp.einsum(
            "ski,sij->skj", operator_spread_in, local_inverse, preferred_element_type=jnp.float32
        )
        corner_terms = jnp.einsum(
            "ski,sci->ksc", operator_spread_in, corner_coupling, preferred_element_type=jnp.float32
        )
        scattered = (
            jnp.zeros((loads, NC), jnp.float32)
            .at[:, flat_map]
            .add(corner_terms.reshape(loads, subdomains * primal))
        )
        summed = lax.psum(scattered, ("sub", "grp"))
        assembled = lax.dynamic_slice_in_dim(summed, lax.axis_index("sub") * sub_cols, sub_cols, 1)
        forward_part = lax.dot_general(
            assembled.astype(jnp.bfloat16),
            coarse_factor,
            (((1,), (1,)), ((), ())),
            preferred_element_type=jnp.float32,
        )
        forward = sum_over_sub(forward_part.astype(jnp.bfloat16))
        coarse_part = jnp.dot(forward, coarse_factor, preferred_element_type=jnp.float32)
        coarse = lax.psum(coarse_part.astype(jnp.bfloat16), "grp")
        coarse_all = gather_over_sub(coarse)
        picked = coarse_all[:, flat_map].reshape(loads, subdomains, primal)
        correction = jnp.einsum(
            "ksc,sci->ski", picked, corner_coupling, preferred_element_type=jnp.float32
        )
        applied = jumps(local_part + correction)
        curvature = lax.psum(column_sum(direction, applied), ("sub", "grp"))
        step_size = res_dot / curvature
        multipliers = multipliers + step_size[None, :, None] * direction
        residual = residual - step_size[None, :, None] * applied
        precond = precondition(residual)
        new_dot = residual_products(residual, precond)
        direction = precond + (new_dot / res_dot)[None, :, None] * direction
        res_dot = new_dot
    return (multipliers, residual, direction)


def struct(shape, dtype):
    return jax.ShapeDtypeStruct(shape, dtype)


def cost(flops, size):
    return pl.CostEstimate(flops=flops, bytes_accessed=size, transcendentals=0)


def params(mib=16):
    return pltpu.CompilerParams(vmem_limit_bytes=mib * 1024 * 1024)


SMEM = pl.BlockSpec(memory_space=pltpu.SMEM)
VMEM = pl.BlockSpec(memory_space=pltpu.VMEM)
ANY = pl.BlockSpec(memory_space=pl.ANY)


def matmul(left, right):
    return lax.dot_general(left, right, (((1,), (0,)), ((), ())), preferred_element_type=F32)


def matmul_t(left, right):
    return lax.dot_general(left, right, (((1,), (1,)), ((), ())), preferred_element_type=F32)


def partners(axis, first):
    peers = lax.axis_size(axis)
    return [(i, (((i + first) ^ 1) - first) % peers) for i in range(peers)]


def from_neighbours(array):
    return [
        lax.ppermute(array, axis, partners(axis, first))
        for axis, first in (("grp", 0), ("grp", 1), ("sub", 1), ("sub", 0))
    ]


def buffers(sub, grp):
    odd_sub, odd_grp = sub % 2, grp % 2
    sides = [3 + odd_grp, 4 - odd_grp, 2 - odd_sub, 1 + odd_sub]
    places = [4 - odd_sub, 3 + odd_sub, 1 + odd_grp, 2 - odd_grp]
    return sides + places


def exchange(array, axes):
    return lax.all_to_all(array, axes, 0, 0, tiled=True)


def halves(values):
    high = values.astype(BF16)
    return jnp.concatenate([high, (values - high.astype(F32)).astype(BF16)], axis=0)


def wide(ref, subdomain):
    return jnp.concatenate([ref[subdomain * 8 + j] for j in range(8)], axis=1)


def square_copies(matrix, held, arrived):
    copies = [pltpu.make_async_copy(matrix.at[s], held.at[s], arrived.at[s]) for s in range(2)]
    for copy in copies:
        copy.start()
    return copies


def square(values, copies, held, out, sent=None):
    for s in range(2):
        full = halves(wide(values, s))
        copies[s].wait()
        got = matmul(full, held[s])
        got = got[:32] + got[32:]
        for j in range(8):
            block = got[:, j * 128 : j * 128 + 128]
            out[8 * s + j] = block
            if sent is not None:
                sent[8 * s + j] = block.astype(BF16)


SQUARE = [pltpu.VMEM((2, 1024, 1024), BF16), pltpu.SemaphoreType.DMA((2,))]
FULL = struct((16, 32, 128), F32)
TABLE = struct((8, 128), jnp.int32)
TABLE_SCRATCH = [pltpu.SMEM((8, 128), jnp.int32), pltpu.SemaphoreType.DMA(())]
OWN = struct((8, 32, 128), F32)
SENT = struct((16, 32, 128), BF16)


def first_kernel(
    inside, own, near, jump, near1, near2, near3, near4, matrix, table, r, out, sent, first, held, arrived
):
    copies = square_copies(matrix, held, arrived)
    for block in range(16):
        for row in range(4):
            table[row, block] = 0
        table[4, block] = inside[4]
        table[5, block] = own[block % 8]
        table[6, block] = (own[8 + block % 8] > 0).astype(jnp.int32)
    first[...] = jnp.zeros_like(first)
    r[...] = jnp.zeros_like(r)
    for m in range(8):
        block = own[m]

        @pl.when(own[8 + m] > 0)
        def _():
            side = own[8 + m]
            table[0, block] = jnp.where(inside[side - 1] > 0, inside[8 + side], 0)
            table[1, block] = own[16 + m]
            table[2, block] = 1
            table[3, block] = 1
            first[block] = jump[m]
            r[m] = jump[m]

    for k, rows in enumerate((near1, near2, near3, near4)):
        side = inside[5 + k]
        facing = jnp.where(lax.rem(side, 2) == 1, side + 1, side - 1)
        for m in range(8):

            @pl.when((inside[side - 1] > 0) & (near[k, 8 + m] == facing))
            def _():
                block = near[k, 16 + m]
                table[0, block] = k + 1
                table[1, block] = near[k, m]
                table[2, block] = 1
                first[block] = -rows[pl.ds(m * 32, 32), :]

    square(first, copies, held, out, sent)


def set_up(jump, own, inside, matrix):
    rows = jnp.concatenate(
        [jump.reshape(256, 128), jnp.pad(own.astype(F32)[None, :], ((0, 7), (0, 104)))], axis=0
    )
    near = from_neighbours(rows)
    near_links = jnp.stack([n[256, :24] for n in near]).astype(jnp.int32)
    return pl.pallas_call(
        first_kernel,
        out_shape=(TABLE, OWN, FULL, SENT),
        in_specs=[SMEM, SMEM, SMEM] + [VMEM] * 5 + [ANY],
        out_specs=(SMEM, VMEM, VMEM, VMEM),
        scratch_shapes=[pltpu.VMEM((16, 32, 128), F32)] + SQUARE,
        compiler_params=params(),
    )(inside, own, near_links, jump, *near, matrix)


def jumps(table, values, near, out):
    for block in range(16):
        side, far = table[0, block], table[1, block]
        other = jnp.zeros((32, 128), F32)
        for k in range(4):
            other = jnp.where(side == k + 1, near[k][far].astype(F32), other)
        out[block] = jnp.where(table[2, block] > 0, values[block] - other, 0.0)


def diagonal():
    lanes = lax.broadcasted_iota(jnp.int32, (32, 128), 1)
    load = lax.broadcasted_iota(jnp.int32, (32, 128), 0)
    return lanes - load


def own_rows(table, ref):
    return [
        jnp.where(table[6, row] > 0, ref[table[5, row]], 0.0) if ref.shape[0] == 16 else ref[row]
        for row in range(8)
    ]


def product_rows(table, pairs):
    lanes = diagonal()
    rows = [jnp.zeros((32, 128), F32) for _ in range((len(pairs) + 3) // 4)]
    for i, pair in enumerate(pairs):
        left, right = (own_rows(table, ref) for ref in pair)
        total = jnp.zeros((32, 128), F32)
        for one, other in zip(left, right):
            total += one * other
        total = jnp.sum(total, axis=1, keepdims=True)
        rows[i // 4] += jnp.where(lanes == 32 * (i % 4), total, 0.0)
    return [jnp.sum(row, axis=0, keepdims=True) for row in rows]


def by_load(row, count):
    lanes = diagonal()
    return [
        jnp.sum(jnp.where(lanes == 32 * i, row, 0.0), axis=1, keepdims=True) for i in range(count)
    ]


def in_thirds(row):
    index = lax.broadcasted_iota(jnp.int32, (8, 128), 0)
    whole = jnp.zeros((8, 128), F32)
    for i in range(3):
        part = row.astype(BF16).astype(F32)
        whole = jnp.where(index == i, part, whole)
        row = row - part
    return whole


def lane_group():
    return lax.broadcasted_iota(jnp.int32, (8, 128), 1) // 32


def pick(lanes, parts, places):
    out = parts[0]
    for part, place in zip(parts[1:], places[1:]):
        out = jnp.where(lanes == place, part, out)
    return out


def turn(values, groups):
    groups = groups % 4
    return values if groups == 0 else pltpu.roll(values, groups * 32, 1)


def one_hot(columns, first, count):
    listed = jnp.concatenate([columns[first + i : first + i + 1, :] for i in range(count)], axis=1)
    index = lax.broadcasted_iota(jnp.int32, (256, 128 * count), 0).astype(F32).astype(BF16)
    parts = []
    for third in range(3):
        low = listed - 256 * third
        low = jnp.where((low >= 0) & (low < 256), low, -1).astype(F32).astype(BF16)
        parts.append(jnp.where(index == low, jnp.ones((), BF16), jnp.zeros((), BF16)))
    return jnp.concatenate(parts, axis=0)


def one_hot_rows(columns, first, count):
    index = lax.broadcasted_iota(jnp.int32, (128, 768), 1).astype(F32)
    parts = [
        jnp.where(index == columns[:, s : s + 1], 1.0, 0.0).astype(BF16)
        for s in range(first, first + count)
    ]
    return jnp.concatenate(parts, axis=0)


def operator_kernel(pairs, listed, values, n1, n2, n3, n4, matrix, *refs):
    count = 4 if pairs else 0
    vectors, (w, out, sent), sums, (held, arrived, table, known) = (
        refs[:count],
        refs[count : count + 3],
        refs[count + 3 : -4],
        refs[-4:],
    )
    tables = pltpu.make_async_copy(listed, table, known)
    tables.start()
    copies = square_copies(matrix, held, arrived)
    tables.wait()
    jumps(table, values, (n1, n2, n3, n4), w)
    if pairs:
        r, u, s, d = vectors
        wanted = [(r, u), (u, w), (u, s), (d, w)][:pairs]
        sums[0][0] = in_thirds(product_rows(table, wanted)[0])
    square(w, copies, held, out, sent)


def after_operator(pairs, table, surface, near, matrix, vectors=()):
    outs = (FULL, FULL, SENT) + ((struct((1, 8, 128), F32),) if pairs else ())
    return pl.pallas_call(
        functools.partial(operator_kernel, pairs),
        out_shape=outs,
        in_specs=[ANY] + [VMEM] * 5 + [ANY] + [VMEM] * len(vectors),
        out_specs=(VMEM,) * len(outs),
        scratch_shapes=SQUARE + TABLE_SCRATCH,
        compiler_params=params(),
    )(table, surface, *near, matrix, *vectors)


COUPLED = [
    pltpu.VMEM((2, 192, 1024), BF16),
    pltpu.VMEM((384, 1024), BF16),
    pltpu.SemaphoreType.DMA((2,)),
]


def coupled_copies(coupling, place, held, placed, arrived):
    copies = [
        pltpu.make_async_copy(coupling, held, arrived.at[0]),
        pltpu.make_async_copy(place, placed, arrived.at[1]),
    ]
    for copy in copies:
        copy.start()
    return copies


def terms_kernel(
    listed, values, n1, n2, n3, n4, coupling_from, place_from, extra, jumped, out, coupling, place, arrived, table, known
):
    tables = pltpu.make_async_copy(listed, table, known)
    tables.start()
    copies = coupled_copies(coupling_from, place_from, coupling, place, arrived)
    tables.wait()
    jumps(table, values, (n1, n2, n3, n4), jumped)
    g = table[4, 0]
    lanes = lane_group()
    terms = []
    for copy in copies:
        copy.wait()
    for s in range(2):
        got = matmul_t(halves(wide(jumped, s)), coupling[s])
        terms.append((got[:32] + got[32:]).astype(BF16))
    placed = matmul(terms[0], place[:192]) + matmul(terms[1], place[192:])
    at = [lax.rem(g + c, 4) for c in range(4)]
    for block in range(8):
        part = [placed[8 * i : 8 * i + 8, block * 128 : (block + 1) * 128] for i in range(4)]
        turned = [
            turn(pick(lanes, [part[(c + j) % 4] for c in range(4)], at), j) for j in range(4)
        ]
        for c in range(4):
            piece = pick(lanes, [turned[(i - c) % 4] for i in range(4)], at)
            s = block * 4 + c
            more = extra[s if extra.shape[0] > 1 else 0]
            out[pl.ds(s * 64, 64), :] = jnp.concatenate([piece, more] * 4, axis=0).astype(BF16)


def corner_terms(table, surface, near, coupling, place, extra):
    jumped, sent = pl.pallas_call(
        terms_kernel,
        out_shape=(FULL, struct((2048, 128), BF16)),
        in_specs=[ANY] + [VMEM] * 5 + [ANY, ANY, VMEM],
        out_specs=(VMEM, VMEM),
        scratch_shapes=COUPLED + TABLE_SCRATCH,
        compiler_params=params(),
    )(table, surface, *near, coupling, place, extra)
    return jumped, exchange(sent, BOTH)


def source_rows(got, s):
    part = got[pl.ds(s * 64, 64), :].astype(F32)
    return [part[16 * c : 16 * c + 16] for c in range(4)]


def factor_copies(factor, held, arrived, half):
    size = held.shape[1]
    copies = []
    for i in range(2):
        at = pl.multiple_of((half * 2 + i) * size, size)
        copies.append(
            pltpu.make_async_copy(factor.at[pl.ds(at, size), :], held.at[i], arrived.at[i])
        )
        copies[-1].start()
    return copies


def core():
    return lax.rem(lax.axis_index("sub"), 2)


def assemble(got, columns):
    lanes = lane_group()
    group = 8
    by_slot = jnp.transpose(columns[...].astype(F32))
    assembled = jnp.zeros((32, 768), F32)
    for first in range(0, 32, group):
        slots = []
        for s in range(first, first + group):
            part = [rows[:8] for rows in source_rows(got, s)]
            loads = [
                turn(pick(lanes, part, [(i + c) % 4 for c in range(4)]), -i) for i in range(4)
            ]
            slots.append(jnp.concatenate(loads, axis=0).astype(BF16))
        assembled += matmul(jnp.concatenate(slots, axis=1), one_hot_rows(by_slot, first, group))
    return assembled


def forward(assembled, copies, held, out):
    assembled = assembled.astype(BF16)
    chunks = held.shape[1] // 128
    for i in range(2):
        copies[i].wait()
        part = matmul_t(assembled, held[i]).astype(BF16)
        for half in range(2):
            for j in range(chunks):
                row = (half * 24 + i * chunks + j) * 16
                out[pl.ds(row, 16), :] = part[16 * half : 16 * half + 16, j * 128 : j * 128 + 128]


def home_kernel(assembled, factor, out, held, arrived):
    forward(assembled[...], factor_copies(factor, held, arrived, core()), held, out)


def home_forward(assembled, factor):
    return pl.pallas_call(
        home_kernel,
        out_shape=HALF,
        in_specs=[VMEM, ANY],
        out_specs=VMEM,
        scratch_shapes=FETCHED,
        compiler_params=params(),
        cost_estimate=cost(2 * 32 * 768 * 3072, 5000000),
    )(assembled, factor)


def first_forward_kernel(
    got, factor, away, assembled_u, columns, spilled, held, arrived
):
    copies = factor_copies(factor, held, arrived, 1 - core())
    flag = jnp.zeros((1, 128), F32)
    for s in range(32):
        column = jnp.zeros((1, 128), F32)
        for rows in source_rows(got, s):
            column += rows[8:9] + 256.0 * rows[9:10]
            flag = jnp.maximum(flag, rows[10:11])
        columns[s : s + 1, :] = column.astype(jnp.int32)
    spilled[...] = flag
    assembled_u[...] = assemble(got, columns)
    forward(assembled_u[...], copies, held, away)


def next_forward_kernel(first, got, columns, old_u, old_q, old, factor, *refs):
    away, assembled_u, assembled_q, kept, held, arrived = refs
    copies = factor_copies(factor, held, arrived, 1 - core())
    total = jnp.zeros((8, 128), F32)
    for s in range(32):
        for rows in source_rows(got, s):
            total += rows[8:]
    gamma, uw, us, dw = by_load(jnp.sum(total, axis=0, keepdims=True), 4)
    if first:
        beta, delta = jnp.zeros_like(gamma), uw
    else:
        beta = gamma / old[0][:, 0:1]
        delta = uw + beta * (us + dw) + beta * beta * old[1][:, 0:1]
    alpha = gamma / delta
    for i, value in enumerate((gamma, delta, alpha, beta)):
        kept[i] = jnp.broadcast_to(value, (32, 128))
    got_q = assemble(got, columns)
    if not first:
        got_q += beta * old_q[...]
    assembled_q[...] = got_q
    assembled_u[...] = old_u[...] - alpha * got_q
    forward(assembled_u[...], copies, held, away)


FETCHED = [pltpu.VMEM((2, 1536, 768), BF16), pltpu.SemaphoreType.DMA((2,))]
HALF = struct((768, 128), BF16)
SUMS = struct((32, 768), F32)
KEPT = struct((4, 32, 128), F32)


def first_forward(got, factor):
    return pl.pallas_call(
        first_forward_kernel,
        out_shape=(
            HALF,
            SUMS,
            struct((32, 128), jnp.int32),
            struct((1, 128), F32),
        ),
        in_specs=[VMEM, ANY],
        out_specs=(VMEM,) * 4,
        scratch_shapes=FETCHED,
        compiler_params=params(24),
    )(got, factor)


def next_forward(first, got, columns, old_u, old_q, old, factor):
    return pl.pallas_call(
        functools.partial(next_forward_kernel, first),
        out_shape=(HALF, SUMS, SUMS, KEPT),
        in_specs=[VMEM] * 5 + [ANY],
        out_specs=(VMEM,) * 4,
        scratch_shapes=FETCHED,
        compiler_params=params(24),
    )(got, columns, old_u, old_q, old, factor)


def pair_kernel(home, got, out):
    out[...] = (home[...].astype(F32) + got[...].astype(F32)).astype(BF16)


def total_kernel(got, out):
    total = got[pl.ds(0, 48), :].astype(F32)
    for peer in range(1, 16):
        total += got[pl.ds(peer * 48, 48), :].astype(F32)
    total = total.astype(BF16)
    for peer in range(16):
        out[pl.ds(peer * 48, 48), :] = total


def coarse_half(got, copies, held):
    chunks = held.shape[1] // 128
    solution = jnp.zeros((32, 768), F32)
    for i in range(2):
        parts = [
            [got[pl.ds((half * 24 + i * chunks + j) * 16, 16), :] for j in range(chunks)]
            for half in range(2)
        ]
        rows = jnp.concatenate([jnp.concatenate(part, axis=1) for part in parts], axis=0)
        copies[i].wait()
        solution += matmul(rows, held[i])
    return solution


def home_coarse_kernel(got, factor, out, held, arrived):
    out[...] = coarse_half(got, factor_copies(factor, held, arrived, core()), held)


def coarse_kernel(got, begun, factor, columns, out, held, arrived):
    copies = factor_copies(factor, held, arrived, 1 - core())
    solution = begun[...] + coarse_half(got, copies, held)
    solution = solution.astype(BF16)
    lanes = lane_group()
    for first in range(0, 32, 8):
        picked = matmul(solution, one_hot(columns, first, 8))
        for s in range(8):
            part = [
                turn(picked[8 * i : 8 * i + 8, s * 128 : s * 128 + 128], i) for i in range(4)
            ]
            pieces = [pick(lanes, part, [(i + c) % 4 for i in range(4)]) for c in range(4)]
            out[pl.ds((first + s) * 32, 32), :] = jnp.concatenate(pieces, axis=0).astype(BF16)


def correct_kernel(
    got, place_from, coupling_from, local, out, sent, coupling, place, arrived
):
    copies = coupled_copies(coupling_from, place_from, coupling, place, arrived)
    g = lax.axis_index("grp")
    lanes = lane_group()
    at = [lax.rem(g + c, 4) for c in range(4)]
    picked = []
    for block in range(8):
        sums = []
        for c in range(4):
            part = got[pl.ds((block * 4 + c) * 32, 32), :].astype(F32)
            sums.append(part[0:8] + part[8:16] + part[16:24] + part[24:32])
        turned = [
            turn(pick(lanes, [sums[(i - j) % 4] for i in range(4)], at), -j) for j in range(4)
        ]
        loads = [pick(lanes, [turned[(i - c) % 4] for c in range(4)], at) for i in range(4)]
        picked.append(jnp.concatenate(loads, axis=0).astype(BF16))
    picked = jnp.concatenate(picked, axis=1)
    for copy in copies:
        copy.wait()
    for s in range(2):
        values = matmul_t(picked, place[192 * s : 192 * s + 192]).astype(BF16)
        correction = matmul(values, coupling[s])
        for j in range(8):
            block = local[8 * s + j] + correction[:, 128 * j : 128 * j + 128]
            out[8 * s + j] = block
            sent[8 * s + j] = block.astype(BF16)


def local_kernel(values, matrix, out, held, arrived):
    square(values, square_copies(matrix, held, arrived), held, out)


def local_part(values, matrix):
    return pl.pallas_call(
        local_kernel,
        out_shape=FULL,
        in_specs=[VMEM, ANY],
        out_specs=VMEM,
        scratch_shapes=SQUARE,
        compiler_params=params(),
        cost_estimate=cost(2 * 64 * 2 * 1024 * 1024, 4800000),
    )(values, matrix)


def small_call(kernel, *args):
    return pl.pallas_call(
        kernel,
        out_shape=HALF,
        in_specs=[VMEM] * len(args),
        out_specs=VMEM,
        compiler_params=params(),
    )(*args)


def operate(away, sums, local, columns, factor, place, coupling):
    peers = lax.axis_size("sub")
    swap = partners("sub", 0)
    kinds = [list(range(first, peers, 2)) for first in range(2)]
    got = lax.ppermute(away, "sub", swap)
    summed = small_call(pair_kernel, home_forward(sums, factor), got)
    got = lax.all_to_all(summed, "sub", 0, 0, axis_index_groups=kinds, tiled=True)
    summed = small_call(total_kernel, got)
    home = lax.all_to_all(summed, "sub", 0, 0, axis_index_groups=kinds, tiled=True)
    other = lax.ppermute(home, "sub", swap)
    begun = pl.pallas_call(
        home_coarse_kernel,
        out_shape=SUMS,
        in_specs=[VMEM, ANY],
        out_specs=VMEM,
        scratch_shapes=FETCHED,
        compiler_params=params(),
        cost_estimate=cost(2 * 32 * 768 * 3072, 5000000),
    )(home, factor)
    coarse = pl.pallas_call(
        coarse_kernel,
        out_shape=struct((1024, 128), BF16),
        in_specs=[VMEM, VMEM, ANY, VMEM],
        out_specs=VMEM,
        scratch_shapes=FETCHED,
        compiler_params=params(24),
    )(other, begun, factor, columns)
    got = exchange(coarse, BOTH)
    return pl.pallas_call(
        correct_kernel,
        out_shape=(FULL, SENT),
        in_specs=[VMEM, ANY, ANY, VMEM],
        out_specs=(VMEM, VMEM),
        scratch_shapes=COUPLED,
        compiler_params=params(),
    )(got, place, coupling, local)


def first_update_kernel(table, kept, r, u, w, m, x_out, r_out, d_out, s_out, u_out):
    alpha = kept[2]
    own_u, own_w = own_rows(table, u), own_rows(table, w)
    for row in range(8):
        d_out[row] = own_u[row]
        s_out[row] = own_w[row]
        x_out[row] = alpha * own_u[row]
        r_out[row] = r[row] - alpha * own_w[row]
    for b in range(16):
        u_out[b] = u[b] - alpha * m[b]


def update_kernel(
    table, kept, x, r, d, s, u, w, m, q, x_out, r_out, d_out, s_out, u_out, q_out
):
    alpha, beta = kept[2], kept[3]
    own_u, own_w = own_rows(table, u), own_rows(table, w)
    for row in range(8):
        dn = own_u[row] + beta * d[row]
        sn = own_w[row] + beta * s[row]
        d_out[row] = dn
        s_out[row] = sn
        x_out[row] = x[row] + alpha * dn
        r_out[row] = r[row] - alpha * sn
    for b in range(16):
        qn = m[b] + beta * q[b]
        q_out[b] = qn
        u_out[b] = u[b] - alpha * qn


def last_products_kernel(
    table, values, n1, n2, n3, n4, r, d, s, u, w, q, own_u, own_w, own_m, own_q, out, m
):
    jumps(table, values, (n1, n2, n3, n4), m)
    pairs = [(r, u), (u, w), (u, s), (d, w), (r, m), (r, q), (w, m), (w, q), (s, m), (s, q)]
    rows = product_rows(table, pairs)
    for kept, ref in ((own_u, u), (own_w, w), (own_m, m), (own_q, q)):
        for i, row in enumerate(own_rows(table, ref)):
            kept[i] = row
    place = lax.rem(lax.broadcasted_iota(jnp.int32, out.shape, 0), 4)
    whole = jnp.zeros(out.shape, F32)
    for i, row in enumerate(rows):
        whole = jnp.where(place == i, row, whole)
    out[...] = whole


def finish_kernel(got, old, x, r, d, s, own_u, own_w, own_m, own_q, x_out, r_out, d_out):
    place = lax.rem(lax.broadcasted_iota(jnp.int32, got.shape, 0), 4)
    totals = []
    for i in range(3):
        totals += by_load(
            jnp.sum(jnp.where(place == i, got[...], 0.0), axis=0, keepdims=True), 4
        )
    gamma, uw, us, dw, rm, rq, wm, wq, sm, sq = totals[:10]
    beta = gamma / old[0][:, 0:1]
    delta = uw + beta * (us + dw) + beta * beta * old[1][:, 0:1]
    alpha = gamma / delta
    cross = rm + beta * rq + uw + beta * us
    squared = wm + beta * (wq + sm) + beta * beta * sq
    last = (gamma - alpha * cross + alpha * alpha * squared) / gamma
    for row in range(8):
        dn = own_u[row] + beta * d[row]
        x_out[row] = x[row] + alpha * dn
        r_out[row] = r[row] - alpha * (own_w[row] + beta * s[row])
        d_out[row] = own_u[row] - alpha * (own_m[row] + beta * own_q[row]) + last * dn


def fast_path(jump, local_inverse, schur, coupling, factor, own, inside, place, listing):
    table, r, surface, sent = set_up(jump, own, inside, schur)
    u, got = corner_terms(table, surface, from_neighbours(sent), coupling, place, listing)
    away, sum_u, columns, spilled = first_forward(got, factor)
    local = local_part(u, local_inverse)
    surface, sent = operate(away, sum_u, local, columns, factor, place, coupling)
    w, surface, sent, sums = after_operator(
        2, table, surface, from_neighbours(sent), schur, (r, u, r, r)
    )
    m, got = corner_terms(table, surface, from_neighbours(sent), coupling, place, sums)
    kept = jnp.zeros(KEPT.shape, F32)
    away, sum_u, sum_q, kept = next_forward(True, got, columns, sum_u, sum_u, kept, factor)
    q = m
    x, r, d, s, u = pl.pallas_call(
        first_update_kernel,
        out_shape=(OWN,) * 4 + (FULL,),
        in_specs=[SMEM] + [VMEM] * 5,
        compiler_params=params(),
    )(table, kept, r, u, w, m)
    local = local_part(u, local_inverse)
    surface, sent = operate(away, sum_u, local, columns, factor, place, coupling)
    w, surface, sent, sums = after_operator(
        4, table, surface, from_neighbours(sent), schur, (r, u, s, d)
    )
    m, got = corner_terms(table, surface, from_neighbours(sent), coupling, place, sums)
    away, sum_u, _, kept = next_forward(False, got, columns, sum_u, sum_q, kept, factor)
    x, r, d, s, u, q = pl.pallas_call(
        update_kernel,
        out_shape=(OWN,) * 4 + (FULL,) * 2,
        in_specs=[SMEM] + [VMEM] * 9,
        compiler_params=params(),
    )(table, kept, x, r, d, s, u, w, m, q)
    local = local_part(u, local_inverse)
    surface, sent = operate(away, sum_u, local, columns, factor, place, coupling)
    w, surface, sent = after_operator(0, table, surface, from_neighbours(sent), schur)
    *kept_rows, sums = pl.pallas_call(
        last_products_kernel,
        out_shape=(OWN,) * 4 + (struct((512, 128), F32),),
        in_specs=[SMEM] + [VMEM] * 11,
        out_specs=(VMEM,) * 5,
        scratch_shapes=[pltpu.VMEM((16, 32, 128), F32)],
        compiler_params=params(),
    )(table, surface, *from_neighbours(sent), r, d, s, u, w, q)
    got = exchange(sums, BOTH)
    outputs = pl.pallas_call(
        finish_kernel,
        out_shape=(OWN,) * 3,
        in_specs=[VMEM] * 10,
        compiler_params=params(),
    )(got, kept, x, r, d, s, *kept_rows)
    return jnp.max(spilled) > 0, outputs


def on_device(
    jump_load,
    local_inverse,
    dirichlet_schur,
    corner_coupling,
    corner_map,
    coarse_factor,
    block_links,
    block_counts,
):
    sub_cols = coarse_factor.shape[1]
    n_sub, n_grp = lax.axis_size("sub"), lax.axis_size("grp")
    sub, grp = lax.axis_index("sub"), lax.axis_index("grp")
    flat_map = corner_map.reshape(-1)
    block = flat_map // sub_cols
    column = flat_map - block * sub_cols
    order = jnp.arange(flat_map.shape[0], dtype=jnp.int32)
    before = (block[:, None] == block[None, :]) & (order[None, :] < order[:, None])
    rank = jnp.sum(before.astype(jnp.int32), axis=1)
    slot = block * CAP + rank
    fits = rank < CAP
    lane = (block // 4) * 128 + ((block + grp) % 4) * CAP + rank
    slots = jnp.arange(n_sub * CAP, dtype=jnp.int32)
    place = ((lane[:, None] == slots[None, :]) & fits[:, None]).astype(BF16)
    filled = jnp.where((slot[:, None] == slots[None, :]) & fits[:, None], column[:, None] + 1, 0)
    filled = jnp.sum(filled, axis=0).reshape(n_sub, CAP)
    filled = jnp.where(filled > 0, filled - 1, sub_cols)
    here = (jnp.arange(128, dtype=jnp.int32) // CAP == grp)[None, :]
    spilled = jnp.any(~fits).astype(jnp.int32)
    listing = jnp.stack(
        [
            jnp.where(here, jnp.tile(filled % 256, (1, 4)), 0),
            jnp.where(here, jnp.tile(filled // 256, (1, 4)), 0),
            jnp.broadcast_to(spilled, (n_sub, 128)),
        ],
        axis=1,
    )
    listing = jnp.pad(listing, ((0, 0), (0, 5), (0, 0))).astype(F32)
    alive = jnp.arange(8, dtype=jnp.int32) < block_counts[0]
    own = jnp.concatenate(
        [block_links[0, 0], jnp.where(alive, block_links[0, 1], 0), block_links[0, 2]]
    )
    inside = jnp.stack(
        [sub < n_sub - 1, sub > 0, grp < n_grp - 1, grp > 0, grp] + buffers(sub, grp)
    ).astype(jnp.int32)
    spills, outputs = fast_path(
        jump_load,
        local_inverse,
        dirichlet_schur,
        corner_coupling,
        coarse_factor,
        own,
        inside,
        place,
        listing,
    )
    return lax.cond(
        spills,
        lambda: general_path(
            jump_load,
            local_inverse,
            dirichlet_schur,
            corner_coupling,
            corner_map,
            coarse_factor,
            block_links,
            block_counts,
        ),
        lambda: outputs,
    )


def solution(mesh):
    in_specs = (
        P(("sub", "grp"), None, None),
        P(("sub", "grp"), None, None),
        P(("sub", "grp"), None, None),
        P(("sub", "grp"), None, None),
        P(("sub", "grp"), None),
        P("grp", "sub"),
        P(("sub", "grp"), None, None),
        P(("sub", "grp")),
    )
    out_specs = (
        P(("sub", "grp"), None, None),
        P(("sub", "grp"), None, None),
        P(("sub", "grp"), None, None),
    )
    return jax.shard_map(
        on_device, mesh=mesh, in_specs=in_specs, out_specs=out_specs, check_vma=False
    )
```

```python
import functools

import jax
import jax.numpy as jnp
from jax import lax
from jax.experimental import pallas as pl
from jax.experimental.pallas import tpu as pltpu
from jax.sharding import PartitionSpec as P

NC = 24576
ITERS = 3
CAP = 32
BOTH = ("sub", "grp")
BF16 = jnp.bfloat16
F32 = jnp.float32


NEIGHBOUR_SPOTS = ((2, 1), (0, 1), (1, 2), (1, 0))


def extended(array, sides, width):
    for axis, dim in sides:
        peers, length = (lax.axis_size(axis), array.shape[dim])
        up = [(i, (i + 1) % peers) for i in range(peers - 1)]
        down = [(j, i) for i, j in up]
        last = lax.slice_in_dim(array, length - width, length, axis=dim)
        first = lax.slice_in_dim(array, 0, width, axis=dim)
        before = lax.ppermute(last, axis, up)
        after = lax.ppermute(first, axis, down)
        array = jnp.concatenate([before, array, after], axis=dim)
    return array


def shortened(array):

    def short(part):
        return part.astype(jnp.bfloat16) if part.dtype == jnp.float32 else part

    return jax.tree.map(short, array)


def neighbours(padded):
    return [padded[position[0], position[1]] for position in NEIGHBOUR_SPOTS]


def gather_over_sub(array):
    peers = lax.axis_size("sub")
    every = jnp.broadcast_to(array[None], (peers,) + array.shape)
    every = lax.all_to_all(every, "sub", 0, 0, tiled=True)
    return every.transpose(1, 0, 2).reshape(array.shape[0], -1)


def sum_over_sub(array):
    peers = lax.axis_size("sub")
    parts = array.reshape(array.shape[0], peers, -1).transpose(1, 0, 2)
    parts = lax.all_to_all(parts, "sub", 0, 0, tiled=True)
    return gather_over_sub(jnp.sum(parts.astype(jnp.float32), axis=0).astype(array.dtype))


def general_path(
    jump_load,
    local_inverse,
    dirichlet_schur,
    corner_coupling,
    corner_map,
    coarse_factor,
    block_links,
    block_counts,
):
    capacity = jump_load.shape[0]
    loads = jump_load.shape[1]
    block_width = jump_load.shape[2]
    subdomains = local_inverse.shape[0]
    interface = local_inverse.shape[1]
    per_sub = interface // block_width
    primal = corner_coupling.shape[1]
    sub_cols = coarse_factor.shape[1]
    alive = jnp.arange(capacity, dtype=jnp.int32) < block_counts[0]
    own_blocks = block_links[0, 0]
    heading = jnp.where(alive, block_links[0, 1], 0)
    far_blocks = block_links[0, 2]
    own_weight = alive.astype(jnp.float32)[:, None, None]
    has_far = (heading > 0).astype(jnp.float32)[:, None, None]
    listing = jnp.stack([heading, far_blocks])
    listed = extended(listing[None, None], (("sub", 0), ("grp", 1)), 1)
    facing = jnp.array([2, 1, 4, 3], jnp.int32)
    near_lists = jnp.stack(neighbours(listed))
    in_rows = near_lists[:, 1, :].reshape(-1)
    in_weight = (
        (near_lists[:, 0, :] == facing[:, None]).astype(jnp.float32).reshape(-1)[:, None, None]
    )
    flat_map = corner_map.reshape(-1)

    def spread(values):
        padded = extended(shortened(values[None, None]), (("sub", 0), ("grp", 1)), 1)
        incoming = jnp.concatenate(neighbours(padded), axis=0)
        summed_up = jnp.zeros((subdomains, loads, per_sub, block_width), jnp.float32)
        summed_up = summed_up.at[own_blocks // per_sub, :, own_blocks % per_sub].add(
            values * own_weight
        )
        summed_up = summed_up.at[in_rows // per_sub, :, in_rows % per_sub].add(
            -incoming * in_weight
        )
        return summed_up.reshape(subdomains, loads, interface).astype(jnp.bfloat16)

    def jumps(surface):
        pieces = surface.reshape(subdomains, loads, per_sub, block_width)
        padded = extended(
            pieces[None, None].astype(jnp.bfloat16), (("sub", 0), ("grp", 1)), 1
        ).astype(jnp.float32)
        nearby = jnp.stack([pieces] + neighbours(padded))
        far_values = nearby[heading, far_blocks // per_sub, :, far_blocks % per_sub]
        own_values = pieces[own_blocks // per_sub, :, own_blocks % per_sub]
        return (own_values - far_values * has_far) * own_weight

    def precondition(residual):
        spread_in = spread(residual)
        return jumps(
            jnp.einsum(
                "ski,sij->skj", spread_in, dirichlet_schur, preferred_element_type=jnp.float32
            )
        )

    def column_sum(left, right):
        return jnp.sum(left * right, axis=(0, 2))

    def residual_products(residual, precond):
        return lax.psum(column_sum(residual, precond), ("sub", "grp"))

    residual = jump_load * own_weight
    multipliers = jnp.zeros_like(residual)
    precond = precondition(residual)
    direction = precond
    res_dot = residual_products(residual, precond)
    for iteration in range(ITERS):
        operator_spread_in = spread(direction)
        local_part = jnp.einsum(
            "ski,sij->skj", operator_spread_in, local_inverse, preferred_element_type=jnp.float32
        )
        corner_terms = jnp.einsum(
            "ski,sci->ksc", operator_spread_in, corner_coupling, preferred_element_type=jnp.float32
        )
        scattered = (
            jnp.zeros((loads, NC), jnp.float32)
            .at[:, flat_map]
            .add(corner_terms.reshape(loads, subdomains * primal))
        )
        summed = lax.psum(scattered, ("sub", "grp"))
        assembled = lax.dynamic_slice_in_dim(summed, lax.axis_index("sub") * sub_cols, sub_cols, 1)
        forward_part = lax.dot_general(
            assembled.astype(jnp.bfloat16),
            coarse_factor,
            (((1,), (1,)), ((), ())),
            preferred_element_type=jnp.float32,
        )
        forward = sum_over_sub(forward_part.astype(jnp.bfloat16))
        coarse_part = jnp.dot(forward, coarse_factor, preferred_element_type=jnp.float32)
        coarse = lax.psum(coarse_part.astype(jnp.bfloat16), "grp")
        coarse_all = gather_over_sub(coarse)
        picked = coarse_all[:, flat_map].reshape(loads, subdomains, primal)
        correction = jnp.einsum(
            "ksc,sci->ski", picked, corner_coupling, preferred_element_type=jnp.float32
        )
        applied = jumps(local_part + correction)
        curvature = lax.psum(column_sum(direction, applied), ("sub", "grp"))
        step_size = res_dot / curvature
        multipliers = multipliers + step_size[None, :, None] * direction
        residual = residual - step_size[None, :, None] * applied
        precond = precondition(residual)
        new_dot = residual_products(residual, precond)
        direction = precond + (new_dot / res_dot)[None, :, None] * direction
        res_dot = new_dot
    return (multipliers, residual, direction)


def struct(shape, dtype):
    return jax.ShapeDtypeStruct(shape, dtype)


def cost(flops, size):
    return pl.CostEstimate(flops=flops, bytes_accessed=size, transcendentals=0)


def params(mib=16):
    return pltpu.CompilerParams(vmem_limit_bytes=mib * 1024 * 1024)


SMEM = pl.BlockSpec(memory_space=pltpu.SMEM)
VMEM = pl.BlockSpec(memory_space=pltpu.VMEM)
ANY = pl.BlockSpec(memory_space=pl.ANY)


def matmul(left, right):
    return lax.dot_general(left, right, (((1,), (0,)), ((), ())), preferred_element_type=F32)


def matmul_t(left, right):
    return lax.dot_general(left, right, (((1,), (1,)), ((), ())), preferred_element_type=F32)


def partners(axis, first):
    peers = lax.axis_size(axis)
    return [(i, (((i + first) ^ 1) - first) % peers) for i in range(peers)]


def from_neighbours(array):
    return [
        lax.ppermute(array, axis, partners(axis, first))
        for axis, first in (("grp", 0), ("grp", 1), ("sub", 1), ("sub", 0))
    ]


def buffers(sub, grp):
    odd_sub, odd_grp = sub % 2, grp % 2
    sides = [3 + odd_grp, 4 - odd_grp, 2 - odd_sub, 1 + odd_sub]
    places = [4 - odd_sub, 3 + odd_sub, 1 + odd_grp, 2 - odd_grp]
    return sides + places


def exchange(array, axes):
    return lax.all_to_all(array, axes, 0, 0, tiled=True)


def halves(values):
    high = values.astype(BF16)
    return jnp.concatenate([high, (values - high.astype(F32)).astype(BF16)], axis=0)


def wide(ref, subdomain):
    return jnp.concatenate([ref[subdomain * 8 + j] for j in range(8)], axis=1)


def square_copies(matrix, held, arrived):
    copies = [pltpu.make_async_copy(matrix.at[s], held.at[s], arrived.at[s]) for s in range(2)]
    for copy in copies:
        copy.start()
    return copies


def square(values, copies, held, out, sent=None):
    for s in range(2):
        full = halves(wide(values, s))
        copies[s].wait()
        got = matmul(full, held[s])
        got = got[:32] + got[32:]
        for j in range(8):
            block = got[:, j * 128 : j * 128 + 128]
            out[8 * s + j] = block
            if sent is not None:
                sent[8 * s + j] = block.astype(BF16)


SQUARE = [pltpu.VMEM((2, 1024, 1024), BF16), pltpu.SemaphoreType.DMA((2,))]
FULL = struct((16, 32, 128), F32)
TABLE = struct((8, 128), jnp.int32)
TABLE_SCRATCH = [pltpu.SMEM((8, 128), jnp.int32), pltpu.SemaphoreType.DMA(())]
OWN = struct((8, 32, 128), F32)
SENT = struct((16, 32, 128), BF16)


def first_kernel(
    inside, own, near, jump, near1, near2, near3, near4, matrix, table, r, out, sent, first, held, arrived
):
    copies = square_copies(matrix, held, arrived)
    for block in range(16):
        for row in range(4):
            table[row, block] = 0
        table[4, block] = inside[4]
        table[5, block] = own[block % 8]
        table[6, block] = (block % 8 < own[24]).astype(jnp.int32)
    first[...] = jnp.zeros_like(first)
    r[...] = jnp.zeros_like(r)
    for m in range(8):
        block = own[m]

        @pl.when(m < own[24])
        def _():
            side = own[8 + m]
            table[0, block] = jnp.where(inside[side - 1] > 0, inside[8 + side], 0)
            table[1, block] = own[16 + m]
            table[2, block] = 1
            table[3, block] = 1
            first[block] = jump[m]
            r[m] = jump[m]

    for k, rows in enumerate((near1, near2, near3, near4)):
        side = inside[5 + k]
        facing = jnp.where(lax.rem(side, 2) == 1, side + 1, side - 1)
        for m in range(8):

            @pl.when((inside[side - 1] > 0) & (m < near[k, 24]) & (near[k, 8 + m] == facing))
            def _():
                block = near[k, 16 + m]
                table[0, block] = k + 1
                table[1, block] = near[k, m]
                table[2, block] = 1
                first[block] = -rows[pl.ds(m * 32, 32), :]

    square(first, copies, held, out, sent)


def set_up(jump, own, inside, matrix):
    rows = jnp.concatenate(
        [jump.reshape(256, 128), jnp.pad(own.astype(F32)[None, :], ((0, 7), (0, 103)))], axis=0
    )
    near = from_neighbours(rows)
    near_links = jnp.stack([n[256, :25] for n in near]).astype(jnp.int32)
    return pl.pallas_call(
        first_kernel,
        out_shape=(TABLE, OWN, FULL, SENT),
        in_specs=[SMEM, SMEM, SMEM] + [VMEM] * 5 + [ANY],
        out_specs=(SMEM, VMEM, VMEM, VMEM),
        scratch_shapes=[pltpu.VMEM((16, 32, 128), F32)] + SQUARE,
        compiler_params=params(),
    )(inside, own, near_links, jump, *near, matrix)


def jumps(table, values, near, out):
    for block in range(16):
        side, far = table[0, block], table[1, block]
        other = jnp.zeros((32, 128), F32)
        for k in range(4):
            other = jnp.where(side == k + 1, near[k][far].astype(F32), other)
        out[block] = jnp.where(table[2, block] > 0, values[block] - other, 0.0)


def diagonal():
    lanes = lax.broadcasted_iota(jnp.int32, (32, 128), 1)
    load = lax.broadcasted_iota(jnp.int32, (32, 128), 0)
    return lanes - load


def own_rows(table, ref):
    return [
        jnp.where(table[6, row] > 0, ref[table[5, row]], 0.0) if ref.shape[0] == 16 else ref[row]
        for row in range(8)
    ]


def product_rows(table, pairs):
    lanes = diagonal()
    rows = [jnp.zeros((32, 128), F32) for _ in range((len(pairs) + 3) // 4)]
    for i, pair in enumerate(pairs):
        left, right = (own_rows(table, ref) for ref in pair)
        total = jnp.zeros((32, 128), F32)
        for one, other in zip(left, right):
            total += one * other
        total = jnp.sum(total, axis=1, keepdims=True)
        rows[i // 4] += jnp.where(lanes == 32 * (i % 4), total, 0.0)
    return [jnp.sum(row, axis=0, keepdims=True) for row in rows]


def by_load(row, count):
    lanes = diagonal()
    return [
        jnp.sum(jnp.where(lanes == 32 * i, row, 0.0), axis=1, keepdims=True) for i in range(count)
    ]


def in_thirds(row):
    index = lax.broadcasted_iota(jnp.int32, (8, 128), 0)
    whole = jnp.zeros((8, 128), F32)
    for i in range(3):
        part = row.astype(BF16).astype(F32)
        whole = jnp.where(index == i, part, whole)
        row = row - part
    return whole


def lane_group():
    return lax.broadcasted_iota(jnp.int32, (8, 128), 1) // 32


def pick(lanes, parts, places):
    out = parts[0]
    for part, place in zip(parts[1:], places[1:]):
        out = jnp.where(lanes == place, part, out)
    return out


def turn(values, groups):
    groups = groups % 4
    return values if groups == 0 else pltpu.roll(values, groups * 32, 1)


def one_hot(columns, first, count):
    listed = jnp.concatenate([columns[first + i : first + i + 1, :] for i in range(count)], axis=1)
    index = lax.broadcasted_iota(jnp.int32, (256, 128 * count), 0).astype(F32).astype(BF16)
    parts = []
    for third in range(3):
        low = listed - 256 * third
        low = jnp.where((low >= 0) & (low < 256), low, -1).astype(F32).astype(BF16)
        parts.append(jnp.where(index == low, jnp.ones((), BF16), jnp.zeros((), BF16)))
    return jnp.concatenate(parts, axis=0)


def one_hot_rows(columns, first, count):
    index = lax.broadcasted_iota(jnp.int32, (128, 768), 1).astype(F32)
    parts = [
        jnp.where(index == columns[:, s : s + 1], 1.0, 0.0).astype(BF16)
        for s in range(first, first + count)
    ]
    return jnp.concatenate(parts, axis=0)


def operator_kernel(pairs, listed, values, n1, n2, n3, n4, matrix, *refs):
    count = 4 if pairs else 0
    vectors, (w, out, sent), sums, (held, arrived, table, known) = (
        refs[:count],
        refs[count : count + 3],
        refs[count + 3 : -4],
        refs[-4:],
    )
    tables = pltpu.make_async_copy(listed, table, known)
    tables.start()
    copies = square_copies(matrix, held, arrived)
    tables.wait()
    jumps(table, values, (n1, n2, n3, n4), w)
    if pairs:
        r, u, s, d = vectors
        wanted = [(r, u), (u, w), (u, s), (d, w)][:pairs]
        sums[0][0] = in_thirds(product_rows(table, wanted)[0])
    square(w, copies, held, out, sent)


def after_operator(pairs, table, surface, near, matrix, vectors=()):
    outs = (FULL, FULL, SENT) + ((struct((1, 8, 128), F32),) if pairs else ())
    return pl.pallas_call(
        functools.partial(operator_kernel, pairs),
        out_shape=outs,
        in_specs=[ANY] + [VMEM] * 5 + [ANY] + [VMEM] * len(vectors),
        out_specs=(VMEM,) * len(outs),
        scratch_shapes=SQUARE + TABLE_SCRATCH,
        compiler_params=params(),
    )(table, surface, *near, matrix, *vectors)


COUPLED = [
    pltpu.VMEM((2, 192, 1024), BF16),
    pltpu.VMEM((384, 1024), BF16),
    pltpu.SemaphoreType.DMA((2,)),
]


def coupled_copies(coupling, place, held, placed, arrived):
    copies = [
        pltpu.make_async_copy(coupling, held, arrived.at[0]),
        pltpu.make_async_copy(place, placed, arrived.at[1]),
    ]
    for copy in copies:
        copy.start()
    return copies


def terms_kernel(
    listed, values, n1, n2, n3, n4, coupling_from, place_from, extra, jumped, out, coupling, place, arrived, table, known
):
    tables = pltpu.make_async_copy(listed, table, known)
    tables.start()
    copies = coupled_copies(coupling_from, place_from, coupling, place, arrived)
    tables.wait()
    jumps(table, values, (n1, n2, n3, n4), jumped)
    g = table[4, 0]
    lanes = lane_group()
    terms = []
    for copy in copies:
        copy.wait()
    for s in range(2):
        got = matmul_t(halves(wide(jumped, s)), coupling[s])
        terms.append((got[:32] + got[32:]).astype(BF16))
    placed = matmul(terms[0], place[:192]) + matmul(terms[1], place[192:])
    at = [lax.rem(g + c, 4) for c in range(4)]
    for block in range(8):
        part = [placed[8 * i : 8 * i + 8, block * 128 : (block + 1) * 128] for i in range(4)]
        turned = [
            turn(pick(lanes, [part[(c + j) % 4] for c in range(4)], at), j) for j in range(4)
        ]
        for c in range(4):
            piece = pick(lanes, [turned[(i - c) % 4] for i in range(4)], at)
            s = block * 4 + c
            more = extra[s if extra.shape[0] > 1 else 0]
            out[pl.ds(s * 64, 64), :] = jnp.concatenate([piece, more] * 4, axis=0).astype(BF16)


def corner_terms(table, surface, near, coupling, place, extra):
    jumped, sent = pl.pallas_call(
        terms_kernel,
        out_shape=(FULL, struct((2048, 128), BF16)),
        in_specs=[ANY] + [VMEM] * 5 + [ANY, ANY, VMEM],
        out_specs=(VMEM, VMEM),
        scratch_shapes=COUPLED + TABLE_SCRATCH,
        compiler_params=params(),
    )(table, surface, *near, coupling, place, extra)
    return jumped, exchange(sent, BOTH)


def source_rows(got, s):
    part = got[pl.ds(s * 64, 64), :].astype(F32)
    return [part[16 * c : 16 * c + 16] for c in range(4)]


def factor_copies(factor, held, arrived, half):
    size = held.shape[1]
    copies = []
    for i in range(2):
        at = pl.multiple_of((half * 2 + i) * size, size)
        copies.append(
            pltpu.make_async_copy(factor.at[pl.ds(at, size), :], held.at[i], arrived.at[i])
        )
        copies[-1].start()
    return copies


def core():
    return lax.rem(lax.axis_index("sub"), 2)


def assemble(got, columns):
    lanes = lane_group()
    group = 8
    by_slot = jnp.transpose(columns[...].astype(F32))
    assembled = jnp.zeros((32, 768), F32)
    for first in range(0, 32, group):
        slots = []
        for s in range(first, first + group):
            part = [rows[:8] for rows in source_rows(got, s)]
            loads = [
                turn(pick(lanes, part, [(i + c) % 4 for c in range(4)]), -i) for i in range(4)
            ]
            slots.append(jnp.concatenate(loads, axis=0).astype(BF16))
        assembled += matmul(jnp.concatenate(slots, axis=1), one_hot_rows(by_slot, first, group))
    return assembled


def forward(assembled, copies, held, out):
    assembled = assembled.astype(BF16)
    chunks = held.shape[1] // 128
    for i in range(2):
        copies[i].wait()
        part = matmul_t(assembled, held[i]).astype(BF16)
        for half in range(2):
            for j in range(chunks):
                row = (half * 24 + i * chunks + j) * 16
                out[pl.ds(row, 16), :] = part[16 * half : 16 * half + 16, j * 128 : j * 128 + 128]


def home_kernel(assembled, factor, out, held, arrived):
    forward(assembled[...], factor_copies(factor, held, arrived, core()), held, out)


def home_forward(assembled, factor):
    return pl.pallas_call(
        home_kernel,
        out_shape=HALF,
        in_specs=[VMEM, ANY],
        out_specs=VMEM,
        scratch_shapes=FETCHED,
        compiler_params=params(),
        cost_estimate=cost(2 * 32 * 768 * 3072, 5000000),
    )(assembled, factor)


def first_forward_kernel(
    got, factor, away, assembled_u, columns, spilled, held, arrived
):
    copies = factor_copies(factor, held, arrived, 1 - core())
    flag = jnp.zeros((1, 128), F32)
    for s in range(32):
        column = jnp.zeros((1, 128), F32)
        for rows in source_rows(got, s):
            column += rows[8:9] + 256.0 * rows[9:10]
            flag = jnp.maximum(flag, rows[10:11])
        columns[s : s + 1, :] = column.astype(jnp.int32)
    spilled[...] = flag
    assembled_u[...] = assemble(got, columns)
    forward(assembled_u[...], copies, held, away)


def next_forward_kernel(first, got, columns, old_u, old_q, old, factor, *refs):
    away, assembled_u, assembled_q, kept, held, arrived = refs
    copies = factor_copies(factor, held, arrived, 1 - core())
    total = jnp.zeros((8, 128), F32)
    for s in range(32):
        for rows in source_rows(got, s):
            total += rows[8:]
    gamma, uw, us, dw = by_load(jnp.sum(total, axis=0, keepdims=True), 4)
    if first:
        beta, delta = jnp.zeros_like(gamma), uw
    else:
        beta = gamma / old[0][:, 0:1]
        delta = uw + beta * (us + dw) + beta * beta * old[1][:, 0:1]
    alpha = gamma / delta
    for i, value in enumerate((gamma, delta, alpha, beta)):
        kept[i] = jnp.broadcast_to(value, (32, 128))
    got_q = assemble(got, columns)
    if not first:
        got_q += beta * old_q[...]
    assembled_q[...] = got_q
    assembled_u[...] = old_u[...] - alpha * got_q
    forward(assembled_u[...], copies, held, away)


FETCHED = [pltpu.VMEM((2, 1536, 768), BF16), pltpu.SemaphoreType.DMA((2,))]
HALF = struct((768, 128), BF16)
SUMS = struct((32, 768), F32)
KEPT = struct((4, 32, 128), F32)


def first_forward(got, factor):
    return pl.pallas_call(
        first_forward_kernel,
        out_shape=(
            HALF,
            SUMS,
            struct((32, 128), jnp.int32),
            struct((1, 128), F32),
        ),
        in_specs=[VMEM, ANY],
        out_specs=(VMEM,) * 4,
        scratch_shapes=FETCHED,
        compiler_params=params(24),
    )(got, factor)


def next_forward(first, got, columns, old_u, old_q, old, factor):
    return pl.pallas_call(
        functools.partial(next_forward_kernel, first),
        out_shape=(HALF, SUMS, SUMS, KEPT),
        in_specs=[VMEM] * 5 + [ANY],
        out_specs=(VMEM,) * 4,
        scratch_shapes=FETCHED,
        compiler_params=params(24),
    )(got, columns, old_u, old_q, old, factor)


def pair_kernel(home, got, out):
    out[...] = (home[...].astype(F32) + got[...].astype(F32)).astype(BF16)


def total_kernel(got, out):
    total = got[pl.ds(0, 48), :].astype(F32)
    for peer in range(1, 16):
        total += got[pl.ds(peer * 48, 48), :].astype(F32)
    total = total.astype(BF16)
    for peer in range(16):
        out[pl.ds(peer * 48, 48), :] = total


def coarse_half(got, copies, held):
    chunks = held.shape[1] // 128
    solution = jnp.zeros((32, 768), F32)
    for i in range(2):
        parts = [
            [got[pl.ds((half * 24 + i * chunks + j) * 16, 16), :] for j in range(chunks)]
            for half in range(2)
        ]
        rows = jnp.concatenate([jnp.concatenate(part, axis=1) for part in parts], axis=0)
        copies[i].wait()
        solution += matmul(rows, held[i])
    return solution


def home_coarse_kernel(got, factor, out, held, arrived):
    out[...] = coarse_half(got, factor_copies(factor, held, arrived, core()), held)


def coarse_kernel(got, begun, factor, columns, out, held, arrived):
    copies = factor_copies(factor, held, arrived, 1 - core())
    solution = begun[...] + coarse_half(got, copies, held)
    solution = solution.astype(BF16)
    lanes = lane_group()
    for first in range(0, 32, 8):
        picked = matmul(solution, one_hot(columns, first, 8))
        for s in range(8):
            part = [
                turn(picked[8 * i : 8 * i + 8, s * 128 : s * 128 + 128], i) for i in range(4)
            ]
            pieces = [pick(lanes, part, [(i + c) % 4 for i in range(4)]) for c in range(4)]
            out[pl.ds((first + s) * 32, 32), :] = jnp.concatenate(pieces, axis=0).astype(BF16)


def correct_kernel(
    got, place_from, coupling_from, local, out, sent, coupling, place, arrived
):
    copies = coupled_copies(coupling_from, place_from, coupling, place, arrived)
    g = lax.axis_index("grp")
    lanes = lane_group()
    at = [lax.rem(g + c, 4) for c in range(4)]
    picked = []
    for block in range(8):
        sums = []
        for c in range(4):
            part = got[pl.ds((block * 4 + c) * 32, 32), :].astype(F32)
            sums.append(part[0:8] + part[8:16] + part[16:24] + part[24:32])
        turned = [
            turn(pick(lanes, [sums[(i - j) % 4] for i in range(4)], at), -j) for j in range(4)
        ]
        loads = [pick(lanes, [turned[(i - c) % 4] for c in range(4)], at) for i in range(4)]
        picked.append(jnp.concatenate(loads, axis=0).astype(BF16))
    picked = jnp.concatenate(picked, axis=1)
    for copy in copies:
        copy.wait()
    for s in range(2):
        values = matmul_t(picked, place[192 * s : 192 * s + 192]).astype(BF16)
        correction = matmul(values, coupling[s])
        for j in range(8):
            block = local[8 * s + j] + correction[:, 128 * j : 128 * j + 128]
            out[8 * s + j] = block
            sent[8 * s + j] = block.astype(BF16)


def local_kernel(values, matrix, out, held, arrived):
    square(values, square_copies(matrix, held, arrived), held, out)


def local_part(values, matrix):
    return pl.pallas_call(
        local_kernel,
        out_shape=FULL,
        in_specs=[VMEM, ANY],
        out_specs=VMEM,
        scratch_shapes=SQUARE,
        compiler_params=params(),
        cost_estimate=cost(2 * 64 * 2 * 1024 * 1024, 4800000),
    )(values, matrix)


def small_call(kernel, *args):
    return pl.pallas_call(
        kernel,
        out_shape=HALF,
        in_specs=[VMEM] * len(args),
        out_specs=VMEM,
        compiler_params=params(),
    )(*args)


def operate(away, sums, local, columns, factor, place, coupling):
    peers = lax.axis_size("sub")
    swap = partners("sub", 0)
    kinds = [list(range(first, peers, 2)) for first in range(2)]
    got = lax.ppermute(away, "sub", swap)
    summed = small_call(pair_kernel, home_forward(sums, factor), got)
    got = lax.all_to_all(summed, "sub", 0, 0, axis_index_groups=kinds, tiled=True)
    summed = small_call(total_kernel, got)
    home = lax.all_to_all(summed, "sub", 0, 0, axis_index_groups=kinds, tiled=True)
    other = lax.ppermute(home, "sub", swap)
    begun = pl.pallas_call(
        home_coarse_kernel,
        out_shape=SUMS,
        in_specs=[VMEM, ANY],
        out_specs=VMEM,
        scratch_shapes=FETCHED,
        compiler_params=params(),
        cost_estimate=cost(2 * 32 * 768 * 3072, 5000000),
    )(home, factor)
    coarse = pl.pallas_call(
        coarse_kernel,
        out_shape=struct((1024, 128), BF16),
        in_specs=[VMEM, VMEM, ANY, VMEM],
        out_specs=VMEM,
        scratch_shapes=FETCHED,
        compiler_params=params(24),
    )(other, begun, factor, columns)
    got = exchange(coarse, BOTH)
    return pl.pallas_call(
        correct_kernel,
        out_shape=(FULL, SENT),
        in_specs=[VMEM, ANY, ANY, VMEM],
        out_specs=(VMEM, VMEM),
        scratch_shapes=COUPLED,
        compiler_params=params(),
    )(got, place, coupling, local)


def first_update_kernel(table, kept, r, u, w, m, x_out, r_out, d_out, s_out, u_out):
    alpha = kept[2]
    own_u, own_w = own_rows(table, u), own_rows(table, w)
    for row in range(8):
        d_out[row] = own_u[row]
        s_out[row] = own_w[row]
        x_out[row] = alpha * own_u[row]
        r_out[row] = r[row] - alpha * own_w[row]
    for b in range(16):
        u_out[b] = u[b] - alpha * m[b]


def update_kernel(
    table, kept, x, r, d, s, u, w, m, q, x_out, r_out, d_out, s_out, u_out, q_out
):
    alpha, beta = kept[2], kept[3]
    own_u, own_w = own_rows(table, u), own_rows(table, w)
    for row in range(8):
        dn = own_u[row] + beta * d[row]
        sn = own_w[row] + beta * s[row]
        d_out[row] = dn
        s_out[row] = sn
        x_out[row] = x[row] + alpha * dn
        r_out[row] = r[row] - alpha * sn
    for b in range(16):
        qn = m[b] + beta * q[b]
        q_out[b] = qn
        u_out[b] = u[b] - alpha * qn


def last_products_kernel(
    table, values, n1, n2, n3, n4, r, d, s, u, w, q, own_u, own_w, own_m, own_q, out, m
):
    jumps(table, values, (n1, n2, n3, n4), m)
    pairs = [(r, u), (u, w), (u, s), (d, w), (r, m), (r, q), (w, m), (w, q), (s, m), (s, q)]
    rows = product_rows(table, pairs)
    for kept, ref in ((own_u, u), (own_w, w), (own_m, m), (own_q, q)):
        for i, row in enumerate(own_rows(table, ref)):
            kept[i] = row
    place = lax.rem(lax.broadcasted_iota(jnp.int32, out.shape, 0), 4)
    whole = jnp.zeros(out.shape, F32)
    for i, row in enumerate(rows):
        whole = jnp.where(place == i, row, whole)
    out[...] = whole


def finish_kernel(got, old, x, r, d, s, own_u, own_w, own_m, own_q, x_out, r_out, d_out):
    place = lax.rem(lax.broadcasted_iota(jnp.int32, got.shape, 0), 4)
    totals = []
    for i in range(3):
        totals += by_load(
            jnp.sum(jnp.where(place == i, got[...], 0.0), axis=0, keepdims=True), 4
        )
    gamma, uw, us, dw, rm, rq, wm, wq, sm, sq = totals[:10]
    beta = gamma / old[0][:, 0:1]
    delta = uw + beta * (us + dw) + beta * beta * old[1][:, 0:1]
    alpha = gamma / delta
    cross = rm + beta * rq + uw + beta * us
    squared = wm + beta * (wq + sm) + beta * beta * sq
    last = (gamma - alpha * cross + alpha * alpha * squared) / gamma
    for row in range(8):
        dn = own_u[row] + beta * d[row]
        x_out[row] = x[row] + alpha * dn
        r_out[row] = r[row] - alpha * (own_w[row] + beta * s[row])
        d_out[row] = own_u[row] - alpha * (own_m[row] + beta * own_q[row]) + last * dn


def fast_path(jump, local_inverse, schur, coupling, factor, own, inside, place, listing):
    table, r, surface, sent = set_up(jump, own, inside, schur)
    u, got = corner_terms(table, surface, from_neighbours(sent), coupling, place, listing)
    away, sum_u, columns, spilled = first_forward(got, factor)
    local = local_part(u, local_inverse)
    surface, sent = operate(away, sum_u, local, columns, factor, place, coupling)
    w, surface, sent, sums = after_operator(
        2, table, surface, from_neighbours(sent), schur, (r, u, r, r)
    )
    m, got = corner_terms(table, surface, from_neighbours(sent), coupling, place, sums)
    kept = jnp.zeros(KEPT.shape, F32)
    away, sum_u, sum_q, kept = next_forward(True, got, columns, sum_u, sum_u, kept, factor)
    q = m
    x, r, d, s, u = pl.pallas_call(
        first_update_kernel,
        out_shape=(OWN,) * 4 + (FULL,),
        in_specs=[SMEM] + [VMEM] * 5,
        compiler_params=params(),
    )(table, kept, r, u, w, m)
    local = local_part(u, local_inverse)
    surface, sent = operate(away, sum_u, local, columns, factor, place, coupling)
    w, surface, sent, sums = after_operator(
        4, table, surface, from_neighbours(sent), schur, (r, u, s, d)
    )
    m, got = corner_terms(table, surface, from_neighbours(sent), coupling, place, sums)
    away, sum_u, _, kept = next_forward(False, got, columns, sum_u, sum_q, kept, factor)
    x, r, d, s, u, q = pl.pallas_call(
        update_kernel,
        out_shape=(OWN,) * 4 + (FULL,) * 2,
        in_specs=[SMEM] + [VMEM] * 9,
        compiler_params=params(),
    )(table, kept, x, r, d, s, u, w, m, q)
    local = local_part(u, local_inverse)
    surface, sent = operate(away, sum_u, local, columns, factor, place, coupling)
    w, surface, sent = after_operator(0, table, surface, from_neighbours(sent), schur)
    *kept_rows, sums = pl.pallas_call(
        last_products_kernel,
        out_shape=(OWN,) * 4 + (struct((512, 128), F32),),
        in_specs=[SMEM] + [VMEM] * 11,
        out_specs=(VMEM,) * 5,
        scratch_shapes=[pltpu.VMEM((16, 32, 128), F32)],
        compiler_params=params(),
    )(table, surface, *from_neighbours(sent), r, d, s, u, w, q)
    got = exchange(sums, BOTH)
    outputs = pl.pallas_call(
        finish_kernel,
        out_shape=(OWN,) * 3,
        in_specs=[VMEM] * 10,
        compiler_params=params(),
    )(got, kept, x, r, d, s, *kept_rows)
    return jnp.max(spilled) > 0, outputs


def on_device(
    jump_load,
    local_inverse,
    dirichlet_schur,
    corner_coupling,
    corner_map,
    coarse_factor,
    block_links,
    block_counts,
):
    sub_cols = coarse_factor.shape[1]
    n_sub, n_grp = lax.axis_size("sub"), lax.axis_size("grp")
    sub, grp = lax.axis_index("sub"), lax.axis_index("grp")
    flat_map = corner_map.reshape(-1)
    block = flat_map // sub_cols
    column = flat_map - block * sub_cols
    order = jnp.arange(flat_map.shape[0], dtype=jnp.int32)
    before = (block[:, None] == block[None, :]) & (order[None, :] < order[:, None])
    rank = jnp.sum(before.astype(jnp.int32), axis=1)
    slot = block * CAP + rank
    fits = rank < CAP
    lane = (block // 4) * 128 + ((block + grp) % 4) * CAP + rank
    slots = jnp.arange(n_sub * CAP, dtype=jnp.int32)
    place = ((lane[:, None] == slots[None, :]) & fits[:, None]).astype(BF16)
    filled = jnp.where((slot[:, None] == slots[None, :]) & fits[:, None], column[:, None] + 1, 0)
    filled = jnp.sum(filled, axis=0).reshape(n_sub, CAP)
    filled = jnp.where(filled > 0, filled - 1, sub_cols)
    here = (jnp.arange(128, dtype=jnp.int32) // CAP == grp)[None, :]
    spilled = jnp.any(~fits).astype(jnp.int32)
    listing = jnp.stack(
        [
            jnp.where(here, jnp.tile(filled % 256, (1, 4)), 0),
            jnp.where(here, jnp.tile(filled // 256, (1, 4)), 0),
            jnp.broadcast_to(spilled, (n_sub, 128)),
        ],
        axis=1,
    )
    listing = jnp.pad(listing, ((0, 0), (0, 5), (0, 0))).astype(F32)
    own = jnp.concatenate([block_links.reshape(24), block_counts])
    inside = jnp.stack(
        [sub < n_sub - 1, sub > 0, grp < n_grp - 1, grp > 0, grp] + buffers(sub, grp)
    ).astype(jnp.int32)
    spills, outputs = fast_path(
        jump_load,
        local_inverse,
        dirichlet_schur,
        corner_coupling,
        coarse_factor,
        own,
        inside,
        place,
        listing,
    )
    return lax.cond(
        spills,
        lambda: general_path(
            jump_load,
            local_inverse,
            dirichlet_schur,
            corner_coupling,
            corner_map,
            coarse_factor,
            block_links,
            block_counts,
        ),
        lambda: outputs,
    )


def solution(mesh):
    in_specs = (
        P(("sub", "grp"), None, None),
        P(("sub", "grp"), None, None),
        P(("sub", "grp"), None, None),
        P(("sub", "grp"), None, None),
        P(("sub", "grp"), None),
        P("grp", "sub"),
        P(("sub", "grp"), None, None),
        P(("sub", "grp")),
    )
    out_specs = (
        P(("sub", "grp"), None, None),
        P(("sub", "grp"), None, None),
        P(("sub", "grp"), None, None),
    )
    return jax.shard_map(
        on_device, mesh=mesh, in_specs=in_specs, out_specs=out_specs, check_vma=False
    )
```
